128 devices in a mesh: dp: 16 (over y, x_lo, core), tp: 8 (over x_hi, z).
Axes of the slice: x: 4 (x_hi: 2, x_lo: 2; x = x_hi * 2 + x_lo), y: 4, z: 4, core: 2. Of those that a mesh axis runs over, the one named last changes fastest.
Arguments:
- queries: bfloat16 [8192, 8192], P('dp', 'tp'), may hold values from -72 to 72
- kv_pool: bfloat16 [256, 128, 2048], P('dp', None, 'tp'), may hold values from -12 to 12
- span_start: int32 [16], P('dp'), may hold values from 0 to 12, as said below
- page_table: int32 [16, 16], P('dp'), may hold values from 0 to 15, each once within a row
- fire_slope: float32 [32], replicated, may hold values from -6 to 6
- fire_shift: float32 [32], replicated, may hold values from -1 to 1
- fire_mix: float32 [32, 64], P(None, 'tp'), may hold values from -3 to 3
- out_weight: bfloat16 [8192, 8192], P('tp'), may hold values from -0.0625 to 0.0625
Outputs:
- mixed: bfloat16 [8192, 8192], P('dp', 'tp')
The draws below stay inside these ranges and needn't reach their ends.
Inputs may be any that keep to these rules, and one draw needn't show every extreme that they name: Each request's span ends at page span_start + 4 at the latest on page 16, and one request reaches it. `page_table`: each row lists every pool slot of its request once.
All inputs are finite; a program needn't handle non-finite values.
Results may differ from the reference program's by a relative error of at most 0.019.
Values may be sent and summed in bfloat16 or wider, within the bound.
No kernel may reach another device: no remote copies, remote signals or barrier semaphores. Data moves between devices by JAX's collectives and lax.ppermute only.
A program may use at most 128 MiB of HBM per device.

```python
import jax
import jax.numpy as jnp
from jax import lax

D = 8192
HEADS = 64
KV_HEADS = 8
HEAD_DIM = 128
FIRE_WIDTH = 32
PAGE = 128
SPAN = 512
MAX_PAGES = 16
N_DP = 16


def draw_queries(key, part):
    key = jax.random.fold_in(key, 5)
    base = jax.random.truncated_normal(key, -6.0, 6.0, (N_DP, SPAN, HEADS, HEAD_DIM), jnp.float32)
    return base.reshape(N_DP * SPAN, HEADS * HEAD_DIM).astype(jnp.bfloat16)


def draw_kv_pool(key, part):
    key = jax.random.fold_in(key, 9)
    shape_full = (N_DP * MAX_PAGES, PAGE, KV_HEADS, 2, HEAD_DIM)
    base = jax.random.truncated_normal(key, -6.0, 6.0, shape_full, jnp.float32)
    return base.reshape(N_DP * MAX_PAGES, PAGE, KV_HEADS * 2 * HEAD_DIM).astype(jnp.bfloat16)


def draw_span_start(key, part):
    key = jax.random.fold_in(key, 3)
    first_key, second_key = jax.random.split(key)
    top_page = MAX_PAGES - SPAN // PAGE
    raw_draw = jax.random.randint(first_key, (N_DP,), 0, top_page + 1)
    skewed = raw_draw * raw_draw // max(top_page, 1)
    chosen = jax.random.randint(second_key, (), 0, N_DP)
    return jnp.where(jnp.arange(N_DP) == chosen, top_page, skewed).astype(jnp.int32)


def block_levels(own_key, extent, cuts, low, top_value):
    loudness, own = 1.0, jax.random.fold_in(own_key, 6)
    for axis_at, shards_of in cuts:
        steps = jnp.exp(jax.random.uniform(jax.random.fold_in(own, axis_at), (shards_of,), jnp.float32, low / len(cuts), top_value / len(cuts)))
        loudness = loudness * jnp.repeat(steps, extent[axis_at] // shards_of).reshape([-1 if axis == axis_at else 1 for axis in range(len(extent))])
    return loudness


def normal_values(stream_key, dims, spread, most, cuts=(), kind=jnp.bfloat16):
    gain = block_levels(stream_key, dims, cuts, -0.22, 0.18) if cuts else 1.0
    values = jax.random.normal(stream_key, dims, jnp.float32) * spread * gain
    return jnp.minimum(jnp.maximum(values, -most), most).astype(kind)


def setup_inputs(seed: int = 0) -> dict:
    splits = jax.random.split(jax.random.key(seed), 9)
    queries = draw_queries(jax.random.fold_in(splits[8], 71), 0)
    kv_pool = draw_kv_pool(jax.random.fold_in(splits[8], 71), 0)
    span_start = draw_span_start(jax.random.fold_in(splits[8], 71), 0)
    page_table = jax.vmap(lambda own: jax.random.permutation(own, MAX_PAGES))(jax.random.split(splits[3], N_DP)).reshape((N_DP, MAX_PAGES)).astype(jnp.int32)
    fire_slope = normal_values(splits[4], (FIRE_WIDTH,), 2.0, 6.0, (), jnp.float32)
    fire_shift = jnp.clip(jax.random.uniform(splits[5], (FIRE_WIDTH,), jnp.float32, -1.0, 1.0), -1.0, 1.0)
    fire_mix = normal_values(splits[6], (FIRE_WIDTH, HEADS), 0.5, 3.0, ((1, 8),), jnp.float32)
    out_weight = normal_values(splits[7], (HEADS * HEAD_DIM, D), (HEADS * HEAD_DIM) ** -0.5, 0.0625, ((0, 8),))
    return dict(queries=queries, kv_pool=kv_pool, span_start=span_start, page_table=page_table, fire_slope=fire_slope, fire_shift=fire_shift, fire_mix=fire_mix, out_weight=out_weight)


threshold = 32.0
big_negative = -1e30


def fire_bias(query_pos, key_pos, fire_slope, fire_shift, fire_mix):
    distance = jnp.maximum(query_pos[:, None] - key_pos[None, :], 0).astype(jnp.float32)
    norm_scale = jnp.log1p(jnp.maximum(query_pos.astype(jnp.float32), threshold))
    dist_ratio = jnp.log1p(distance) / norm_scale[:, None]
    hidden = jax.nn.relu(dist_ratio[:, :, None] * fire_slope + fire_shift)
    return jnp.einsum("qkf,fh->hqk", hidden, fire_mix, precision=lax.Precision.HIGHEST)


def rank_attention(queries, pool_pages, table_row, start_page, fire_slope, fire_shift, fire_mix):
    row_count = queries.shape[0]
    context = MAX_PAGES * PAGE
    group_size = HEADS // KV_HEADS
    page_tiles = jnp.take(pool_pages, table_row, axis=0).reshape(context, KV_HEADS, 2, HEAD_DIM)
    query_pos = start_page * PAGE + jnp.arange(row_count, dtype=jnp.int32)
    key_pos = jnp.arange(context, dtype=jnp.int32)
    bias = fire_bias(query_pos, key_pos, fire_slope, fire_shift, fire_mix)
    bias = bias.reshape(KV_HEADS, group_size, row_count, context)
    grouped = queries.reshape(row_count, KV_HEADS, group_size, HEAD_DIM).transpose(1, 0, 2, 3)
    key_rows = page_tiles[:, :, 0].transpose(1, 0, 2)
    value_rows = page_tiles[:, :, 1].transpose(1, 0, 2)
    key_mask = key_pos[None, :] <= query_pos[:, None]

    def per_head(operands):
        q_head, k_head, v_head, b_head = operands
        scores = jnp.einsum("rgd,kd->grk", q_head.astype(jnp.float32), k_head.astype(jnp.float32)) * (HEAD_DIM ** -0.5) + b_head
        row_peak = jnp.max(jnp.where(key_mask, scores, big_negative), axis=-1)
        expo = jnp.where(key_mask, jnp.exp(scores - row_peak[..., None]), 0.0)
        row_total = jnp.sum(expo, axis=-1)
        probs = expo.astype(jnp.bfloat16)
        summed = jnp.einsum("grk,kd->grd", probs.astype(jnp.float32), v_head.astype(jnp.float32))
        return summed / row_total[..., None]

    outputs = lax.map(per_head, (grouped, key_rows, value_rows, bias))
    return outputs.transpose(2, 0, 1, 3).reshape(row_count, HEADS * HEAD_DIM).astype(jnp.bfloat16)


def reference(queries, kv_pool, span_start, page_table, fire_slope, fire_shift, fire_mix, out_weight):
    rank_queries = queries.reshape(N_DP, SPAN, HEADS * HEAD_DIM)
    rank_pools = kv_pool.reshape(N_DP, MAX_PAGES, PAGE, KV_HEADS * 2 * HEAD_DIM)

    def one_rank(operands):
        return rank_attention(operands[0], operands[1], operands[2], operands[3], fire_slope, fire_shift, fire_mix)

    attended = lax.map(one_rank, (rank_queries, rank_pools, page_table, span_start))
    attended = attended.reshape(N_DP * SPAN, HEADS * HEAD_DIM)
    return jnp.dot(attended, out_weight, preferred_element_type=jnp.float32).astype(jnp.bfloat16)
```

```python
import functools
import math

import jax
import jax.numpy as jnp
import numpy as np
from jax import lax
from jax.experimental import pallas as pl
from jax.experimental.pallas import tpu as pltpu
from jax.sharding import PartitionSpec as P

HEAD_DIM = 128
PAGE = 128
HEADS = 8
HIDDEN = 32
CHUNK = 128
KEYS = 256
COLUMNS = 1024
CONTEXT = 2048
THRESHOLD = 32
NEG = -1e30
SCALE = HEAD_DIM**-0.5
TO_EXP2 = SCALE * math.log2(math.e)
MIB = 1 << 20


def column_blocks():
    me = lax.axis_index("tp")
    core = lax.rem(lax.axis_index("dp"), 2)
    hi, z = me // 4, lax.rem(me, 4)
    flip, mirror = z + 1 - 2 * lax.rem(z, 2), 3 - z
    first = jnp.where(core == 0, flip, mirror)
    second = jnp.where(core == 0, mirror, flip)
    both = 3 - first
    both = jnp.where(core == 0, 3 - flip, mirror + 1 - 2 * lax.rem(mirror, 2))
    own, other = hi * 4, (1 - hi) * 4
    return [
        own + first, own + both, other + first, other + both,
        other + z, other + second, own + z, own + second,
    ]


def attention(
    chunk, start_ref, table_ref, slope_ref, shift_ref, mix_ref, logs_ref, recs_ref,
    q_ref, kv_ref, mixb_ref, qt, acc, peak, mass, xs, kinks, att,
):
    row0 = (start_ref[0] + chunk) * PAGE
    for h in range(HEADS):
        qt[:, h * 128 : (h + 1) * 128] = q_ref[:, h * 128 : (h + 1) * 128].T
    acc[...] = jnp.zeros_like(acc)
    mass[...] = jnp.zeros_like(mass)
    peak[...] = jnp.full_like(peak, NEG)
    rows = row0 + lax.broadcasted_iota(jnp.int32, (1, CHUNK), 1)
    rec = 1.0 / jnp.log(1.0 + jnp.maximum(rows, THRESHOLD).astype(jnp.float32))
    ahead = lax.broadcasted_iota(jnp.int32, (KEYS, CHUNK), 1) - lax.broadcasted_iota(
        jnp.int32, (KEYS, CHUNK), 0
    )
    tiles = (start_ref[0] + chunk + KEYS // PAGE) // (KEYS // PAGE)

    def tile(b, carry):
        gap = row0 - b * KEYS
        xs[...] = jnp.log(1.0 + jnp.maximum(ahead + gap, 0).astype(jnp.float32)) * rec
        slots = [table_ref[0, b * (KEYS // PAGE) + n] for n in range(KEYS // PAGE)]
        low = logs_ref[jnp.maximum(gap - (KEYS - 1), 0)] * recs_ref[row0 + CHUNK - 1]
        high = logs_ref[gap + CHUNK - 1] * recs_ref[row0]
        low, high = low * (1 - 1e-5), high * (1 + 1e-5)
        bent = jnp.int32(0)
        flat = jnp.zeros((HEADS, CHUNK), jnp.float32)
        steep = jnp.zeros((HEADS, CHUNK), jnp.float32)
        for f in range(HIDDEN):
            slope, shift = slope_ref[f], shift_ref[f]
            at_low, at_high = slope * low + shift, slope * high + shift
            least, most = jnp.minimum(at_low, at_high), jnp.maximum(at_low, at_high)
            kinks[bent] = f
            bent = bent + jnp.where((least < 0) & (most > 0), 1, 0)
            on = least >= 0
            flat = flat + mixb_ref[f] * jnp.where(on, shift, 0.0)
            steep = steep + mixb_ref[f] * jnp.where(on, slope, 0.0)
        k = jnp.concatenate([kv_ref[s, :, :128] for s in slots], axis=0)
        vt = jnp.concatenate([kv_ref[s, :, 128:].T for s in slots], axis=1)

        def heads(full):
            for g in range(HEADS // 2):
                two = jnp.dot(
                    k, qt[:, g * 256 : (g + 1) * 256], preferred_element_type=jnp.float32
                )
                probs, factors = [], []
                for u in range(2):
                    h = 2 * g + u
                    t = two[:, u * 128 : (u + 1) * 128] + steep[h : h + 1] * xs[...]
                    if full:

                        def unit(n, t, h=h):
                            f = kinks[n]
                            relu = jnp.maximum(slope_ref[f] * xs[...] + shift_ref[f], 0.0)
                            return t + (mix_ref[f, h] * (1 / SCALE)) * relu

                        t = lax.fori_loop(0, bent, unit, t)
                        t = jnp.where(ahead + gap >= 0, t, NEG)
                    before = peak[h : h + 1]
                    after = jnp.maximum(
                        before, jnp.max(t, axis=0, keepdims=True) + flat[h : h + 1]
                    )
                    factor = jnp.exp2((before - after) * TO_EXP2)
                    p = jnp.exp2((t - (after - flat[h : h + 1])) * TO_EXP2)
                    mass[h] = mass[h] * factor + jnp.sum(p.reshape(KEYS // 8, 8, CHUNK), axis=0)
                    peak[h : h + 1] = after
                    probs.append(p.astype(jnp.bfloat16))
                    factors.append(factor)
                update = jnp.dot(
                    vt, jnp.concatenate(probs, axis=1), preferred_element_type=jnp.float32
                )
                acc[g] = acc[g] * jnp.concatenate(factors, axis=1) + update

        plain = (bent == 0) & (gap >= KEYS - 1)

        @pl.when(plain)
        def _():
            heads(False)

        @pl.when(jnp.logical_not(plain))
        def _():
            heads(True)

        return carry

    lax.fori_loop(0, tiles, tile, 0)
    for h in range(HEADS):
        total = jnp.sum(mass[h], axis=0, keepdims=True)
        out = acc[h // 2, :, (h % 2) * 128 : (h % 2 + 1) * 128] / total
        att[:, h * 128 : (h + 1) * 128] = out.T.astype(jnp.bfloat16)


def kernel(
    chunk, start_ref, table_ref, slope_ref, shift_ref, mix_ref, logs_ref, recs_ref,
    q_ref, kv_ref, mixb_ref, w_ref, send_ref, cross_ref, keep_ref,
    qt, acc, peak, mass, xs, kinks, att, wbuf, sems,
):
    blocks = column_blocks()

    def fetch(n):
        columns = pl.ds(pl.multiple_of(blocks[n] * COLUMNS, COLUMNS), COLUMNS)
        return pltpu.make_async_copy(w_ref.at[:, columns], wbuf.at[n], sems.at[n])

    for n in range(8):
        fetch(n).start()
    attention(
        chunk, start_ref, table_ref, slope_ref, shift_ref, mix_ref, logs_ref, recs_ref,
        q_ref, kv_ref, mixb_ref, qt, acc, peak, mass, xs, kinks, att,
    )
    for n in range(8):
        fetch(n).wait()
    for ref, first, count in ((send_ref, 0, 4), (cross_ref, 4, 2), (keep_ref, 6, 2)):

        def block(n, carry, ref=ref, first=first):
            ref[n] = jnp.dot(
                att[...], wbuf[first + n], preferred_element_type=jnp.float32
            ).astype(jnp.bfloat16)
            return carry

        lax.fori_loop(0, count, block, 0)


def partial_sums(chunk, start, table, slope, shift, mix, logs, recs, queries, kv, mixb, w):
    smem = pl.BlockSpec(memory_space=pltpu.SMEM)
    return pl.pallas_call(
        functools.partial(kernel, chunk),
        grid=(1,),
        in_specs=[smem] * 7
        + [
            pl.BlockSpec((CHUNK, HEADS * 128), lambda i: (chunk, 0)),
            pl.BlockSpec((16, PAGE, 256), lambda i: (0, 0, 0)),
            pl.BlockSpec((HIDDEN, HEADS, CHUNK), lambda i: (0, 0, 0)),
            pl.BlockSpec(memory_space=pl.ANY),
        ],
        out_specs=[
            pl.BlockSpec((n, CHUNK, COLUMNS), lambda i: (0, 0, 0)) for n in (4, 2, 2)
        ],
        out_shape=[
            jax.ShapeDtypeStruct((n, CHUNK, COLUMNS), jnp.bfloat16) for n in (4, 2, 2)
        ],
        scratch_shapes=[
            pltpu.VMEM((128, HEADS * CHUNK), jnp.bfloat16),
            pltpu.VMEM((HEADS // 2, 128, 2 * CHUNK), jnp.float32),
            pltpu.VMEM((HEADS, CHUNK), jnp.float32),
            pltpu.VMEM((HEADS, 8, CHUNK), jnp.float32),
            pltpu.VMEM((KEYS, CHUNK), jnp.float32),
            pltpu.SMEM((HIDDEN,), jnp.int32),
            pltpu.VMEM((CHUNK, HEADS * 128), jnp.bfloat16),
            pltpu.VMEM((8, HEADS * 128, COLUMNS), jnp.bfloat16),
            pltpu.SemaphoreType.DMA((8,)),
        ],
        compiler_params=pltpu.CompilerParams(vmem_limit_bytes=44 * MIB),
        cost_estimate=pl.CostEstimate(
            flops=2 * CHUNK * 8192 * 1024 * 2, bytes_accessed=24 * MIB, transcendentals=CHUNK * 2048 * 8
        ),
        name=f"chunk{chunk}",
    )(start, table, slope, shift, mix, logs, recs, queries, kv, mixb, w)


def swap(x, step):
    pairs = []
    for dp in range(16):
        for hi in range(2):
            for z in range(4):
                if step == 1:
                    to = (1 - hi) * 4 + z
                else:
                    to = hi * 4 + ((z ^ 1) if (dp + step // 2) % 2 == 0 else 3 - z)
                pairs.append((dp * 8 + hi * 4 + z, dp * 8 + to))
    return lax.ppermute(x, ("dp", "tp"), pairs)


def shards(queries, kv_pool, span_start, page_table, fire_slope, fire_shift, fire_mix, out_weight):
    index = np.arange(CONTEXT)
    logs = jnp.asarray(np.log1p(index).astype(np.float32))
    recs = jnp.asarray((1 / np.log1p(np.maximum(index, THRESHOLD))).astype(np.float32))
    mixb = jnp.broadcast_to((fire_mix * (1 / SCALE))[:, :, None], (HIDDEN, HEADS, CHUNK))
    outs = []
    f32 = jnp.float32
    for chunk in range(queries.shape[0] // CHUNK):
        send, cross, keep = partial_sums(
            chunk, span_start, page_table, fire_slope, fire_shift, fire_mix, logs, recs,
            queries, kv_pool, mixb, out_weight,
        )
        got = swap(send, 0)
        got_x = swap((cross.astype(f32) + got[2:].astype(f32)).astype(jnp.bfloat16), 1)
        part = [keep[n].astype(f32) + got[n].astype(f32) + got_x[n].astype(f32) for n in range(2)]
        got_z = swap(part[1].astype(jnp.bfloat16), 2)
        outs.append((part[0] + got_z.astype(f32)).astype(jnp.bfloat16))
    return jnp.concatenate(outs, axis=0)


def solution(mesh):
    in_specs = (
        P("dp", "tp"),
        P("dp", None, "tp"),
        P("dp"),
        P("dp", None),
        P(),
        P(),
        P(None, "tp"),
        P("tp", None),
    )
    out_specs = P("dp", "tp")
    return jax.shard_map(shards, mesh=mesh, in_specs=in_specs, out_specs=out_specs, check_vma=False)
```

```python
import functools
import math

import jax
import jax.numpy as jnp
from jax import lax
from jax.experimental import pallas as pl
from jax.experimental.pallas import tpu as pltpu
from jax.sharding import PartitionSpec as P

HEAD_DIM = 128
PAGE = 128
HEADS = 8
HIDDEN = 32
CHUNK = 128
KEYS = 256
GROUP = 32
WIDE = HEADS * CHUNK
COLUMNS = 1024
TILES = 2048 // KEYS
THRESHOLD = 32
NEG = -1e30
SCALE = HEAD_DIM**-0.5
TO_EXP2 = SCALE * math.log2(math.e)
MIB = 1 << 20


def column_blocks():
    me = lax.axis_index("tp")
    core = lax.rem(lax.axis_index("dp"), 2)
    hi, z = me // 4, lax.rem(me, 4)
    flip, mirror = z + 1 - 2 * lax.rem(z, 2), 3 - z
    first = jnp.where(core == 0, flip, mirror)
    second = jnp.where(core == 0, mirror, flip)
    both = 3 - first
    both = jnp.where(core == 0, 3 - flip, mirror + 1 - 2 * lax.rem(mirror, 2))
    own, other = hi * 4, (1 - hi) * 4
    return [
        own + first, own + both, other + first, other + both,
        other + z, other + second, own + z, own + second,
    ]


def attention(chunk, params, q_ref, kv_ref, units_ref, qt, acc, peak, mass, scores, probs, scale, xs, lines, bits, kinks, att):
    start_ref, table_ref, fire_ref = params
    row0 = (start_ref[0] + chunk) * PAGE
    for h in range(HEADS):
        qt[:, h * 128 : (h + 1) * 128] = q_ref[:, h * 128 : (h + 1) * 128].T
    acc[...] = jnp.zeros_like(acc)
    mass[...] = jnp.zeros_like(mass)
    peak[...] = jnp.full_like(peak, NEG)
    probs[1][...] = jnp.zeros_like(probs[1])
    scale[1][...] = jnp.zeros_like(scale[1])
    rows = row0 + lax.broadcasted_iota(jnp.int32, (1, CHUNK), 1)
    rec = 1.0 / jnp.log(1.0 + jnp.maximum(rows, THRESHOLD).astype(jnp.float32))
    ahead = lax.broadcasted_iota(jnp.int32, (KEYS, CHUNK), 1) - lax.broadcasted_iota(
        jnp.int32, (KEYS, CHUNK), 0
    )
    pages = KEYS // PAGE
    tiles = (start_ref[0] + chunk + pages) // pages

    def slots(b):
        return [table_ref[0, jnp.minimum(b * pages + n, 15)] for n in range(pages)]

    gaps = row0 - KEYS * lax.broadcasted_iota(jnp.int32, (TILES, 128), 0)
    least_log = jnp.log(1.0 + jnp.maximum(gaps - (KEYS - 1), 0).astype(jnp.float32))
    most_log = jnp.log(1.0 + jnp.maximum(gaps + (CHUNK - 1), 0).astype(jnp.float32))
    low = least_log * (jnp.min(rec, axis=1, keepdims=True) * (1 - 1e-5))
    high = most_log * (jnp.max(rec, axis=1, keepdims=True) * (1 + 1e-5))
    slope, shift, mix = units_ref[0:1], units_ref[1:2], units_ref[8:16]
    at_low, at_high = slope * low + shift, slope * high + shift
    least, most = jnp.minimum(at_low, at_high), jnp.maximum(at_low, at_high)
    unit = lax.broadcasted_iota(jnp.int32, (TILES, 128), 1)
    weight = jnp.left_shift(1, unit & 15).astype(jnp.float32)
    weight = jnp.where((least < 0) & (most > 0), weight, 0.0)
    weights = jnp.where(unit < 16, weight, 0.0), jnp.where(unit < 16, 0.0, weight)
    shift_on, slope_on = jnp.where(least >= 0, shift, 0.0), jnp.where(least >= 0, slope, 0.0)
    for b in range(TILES):
        for n, on in enumerate((shift_on, slope_on)):
            line = jnp.sum(mix * on[b : b + 1], axis=1, keepdims=True)
            lines[b, n] = jnp.broadcast_to(line, (HEADS, CHUNK))
            bits[b, n] = jnp.sum(weights[n][b : b + 1]).astype(jnp.int32)

    def score(b, slot):
        k = jnp.concatenate([kv_ref[s, :, :128] for s in slots(b)], axis=0)
        for g in range(HEADS // 2):
            columns = slice(g * 256, (g + 1) * 256)
            scores[slot][:, columns] = jnp.dot(k, qt[:, columns], preferred_element_type=jnp.float32)
        gap = row0 - b * KEYS
        xs[slot][...] = jnp.log(1.0 + jnp.maximum(ahead + gap, 0).astype(jnp.float32)) * rec

    def mend(b, slot):
        gap = row0 - b * KEYS
        halves = bits[jnp.minimum(b, TILES - 1), 0], bits[jnp.minimum(b, TILES - 1), 1]

        @pl.when((halves[0] + halves[1] > 0) | (gap < KEYS - 1))
        def _():
            bent = jnp.int32(0)
            for f in range(HIDDEN):
                kinks[bent] = f
                bent = bent + (lax.shift_right_logical(halves[f // 16], f % 16) & 1)
            kinks[bent] = HIDDEN

            def group(n, carry):
                at = pl.ds(pl.multiple_of(n * GROUP, GROUP), GROUP)
                x = xs[slot][at, :]

                def unit(e, terms):
                    f, g = kinks[2 * e], kinks[2 * e + 1]
                    one = jnp.maximum(fire_ref[0, f] * x + fire_ref[1, f], 0.0)
                    two = jnp.maximum(fire_ref[0, g] * x + fire_ref[1, g], 0.0)
                    return tuple(
                        t + (fire_ref[8 + h, f] * one + fire_ref[8 + h, g] * two)
                        for h, t in enumerate(terms)
                    )

                terms = tuple(scores[slot][at, h * 128 : (h + 1) * 128] for h in range(HEADS))
                terms = lax.fori_loop(0, (bent + 1) // 2, unit, terms)
                seen = ahead[:GROUP] + (gap - n * GROUP) >= 0
                for h in range(HEADS):
                    scores[slot][at, h * 128 : (h + 1) * 128] = jnp.where(seen, terms[h], NEG)
                return carry

            lax.fori_loop(0, KEYS // GROUP, group, 0)

    def weigh(b, slot):
        b = jnp.minimum(b, TILES - 1)
        for h in range(HEADS):
            columns = slice(h * 128, (h + 1) * 128)
            flat = lines[b, 0, h : h + 1]
            t = scores[slot][:, columns] + lines[b, 1, h : h + 1] * xs[slot][...]
            before = peak[h : h + 1]
            after = jnp.maximum(before, jnp.max(t, axis=0, keepdims=True) + flat)
            factor = jnp.exp2((before - after) * TO_EXP2)
            p = jnp.exp2((t - (after - flat)) * TO_EXP2)
            mass[h] = mass[h] * factor + jnp.sum(p.reshape(KEYS // 8, 8, CHUNK), axis=0)
            peak[h : h + 1] = after
            scale[slot][:, columns] = factor
            probs[slot][:, columns] = p.astype(jnp.bfloat16)

    def gather(b, slot):
        vt = jnp.concatenate([kv_ref[s, :, 128:].T for s in slots(b)], axis=1)
        for g in range(HEADS // 2):
            columns = slice(g * 256, (g + 1) * 256)
            update = jnp.dot(vt, probs[slot][:, columns], preferred_element_type=jnp.float32)
            acc[:, columns] = acc[:, columns] * scale[slot][:, columns] + update

    def step(b, slot):
        mend(b, slot)
        score(b + 1, 1 - slot)
        gather(jnp.maximum(b - 1, 0), 1 - slot)
        weigh(b, slot)

    def tile(b, carry):
        for slot in range(2):
            pl.when(b % 2 == slot)(functools.partial(step, b, slot))
        return carry

    score(0, 0)
    lax.fori_loop(0, tiles, tile, 0)
    for slot in range(2):
        pl.when(tiles % 2 != slot)(functools.partial(gather, tiles - 1, slot))
    for h in range(HEADS):
        columns = slice(h * 128, (h + 1) * 128)
        total = jnp.sum(mass[h], axis=0, keepdims=True)
        att[:, columns] = (acc[:, columns] / total).T.astype(jnp.bfloat16)


def kernel(chunk, *refs):
    params, (units_ref, q_ref, kv_ref, w_ref) = refs[:3], refs[3:7]
    outs, scratch = refs[-23:-20], refs[-20:]
    (
        qt, acc, peak, mass, s0, s1, p0, p1, f0, f1, x0, x1, lines, bits, kinks, att,
        wbuf, stage, fetched, stored,
    ) = scratch
    blocks = column_blocks()

    def fetch(n):
        columns = pl.ds(pl.multiple_of(blocks[n] * COLUMNS, COLUMNS), COLUMNS)
        return pltpu.make_async_copy(w_ref.at[:, columns], wbuf.at[n], fetched.at[n])

    for n in range(8):
        fetch(n).start()
    attention(
        chunk, params, q_ref, kv_ref, units_ref, qt, acc, peak, mass,
        (s0, s1), (p0, p1), (f0, f1), (x0, x1), lines, bits, kinks, att,
    )
    for n in range(8):
        fetch(n).wait()

    def block(n, carry):
        stage[n] = jnp.dot(att[...], wbuf[n], preferred_element_type=jnp.float32).astype(jnp.bfloat16)
        return carry

    copies = []
    for n, (ref, first, count) in enumerate(zip(outs, (0, 4, 6), (4, 2, 2))):
        lax.fori_loop(first, first + count, block, 0)
        copies.append(pltpu.make_async_copy(stage.at[first : first + count], ref, stored.at[n]))
        copies[-1].start()
    for copy in copies:
        copy.wait()


def partial_sums(chunk, start, table, units, queries, kv, w, after=()):
    smem = pl.BlockSpec(memory_space=pltpu.SMEM)
    return pl.pallas_call(
        functools.partial(kernel, chunk),
        grid=(1,),
        in_specs=[smem] * 3
        + [
            pl.BlockSpec((16, 128), lambda i: (0, 0)),
            pl.BlockSpec((CHUNK, HEADS * 128), lambda i: (chunk, 0)),
            pl.BlockSpec((16, PAGE, 256), lambda i: (0, 0, 0)),
        ]
        + [pl.BlockSpec(memory_space=pl.ANY)] * (1 + len(after)),
        out_specs=[pl.BlockSpec(memory_space=pl.ANY)] * 3,
        out_shape=[
            jax.ShapeDtypeStruct((n, CHUNK, COLUMNS), jnp.bfloat16) for n in (4, 2, 2)
        ],
        scratch_shapes=[
            pltpu.VMEM((128, WIDE), jnp.bfloat16),
            pltpu.VMEM((128, WIDE), jnp.float32),
            pltpu.VMEM((HEADS, CHUNK), jnp.float32),
            pltpu.VMEM((HEADS, 8, CHUNK), jnp.float32),
        ]
        + [pltpu.VMEM((KEYS, WIDE), jnp.float32)] * 2
        + [pltpu.VMEM((KEYS, WIDE), jnp.bfloat16)] * 2
        + [pltpu.VMEM((1, WIDE), jnp.float32)] * 2
        + [pltpu.VMEM((KEYS, CHUNK), jnp.float32)] * 2
        + [
            pltpu.VMEM((TILES, 2, HEADS, CHUNK), jnp.float32),
            pltpu.SMEM((TILES, 2), jnp.int32),
            pltpu.SMEM((HIDDEN + 1,), jnp.int32),
            pltpu.VMEM((CHUNK, HEADS * 128), jnp.bfloat16),
            pltpu.VMEM((8, HEADS * 128, COLUMNS), jnp.bfloat16),
            pltpu.VMEM((8, CHUNK, COLUMNS), jnp.bfloat16),
            pltpu.SemaphoreType.DMA((8,)),
            pltpu.SemaphoreType.DMA((3,)),
        ],
        compiler_params=pltpu.CompilerParams(vmem_limit_bytes=60 * MIB),
        cost_estimate=pl.CostEstimate(
            flops=12 * 10**9, bytes_accessed=20 * MIB, transcendentals=CHUNK * 2048 * 8
        ),
        name=f"chunk{chunk}",
    )(start, table, units, units, queries, kv, w, *after)


def swap(x, step):
    pairs = []
    for dp in range(16):
        for hi in range(2):
            for z in range(4):
                if step == 1:
                    to = (1 - hi) * 4 + z
                else:
                    to = hi * 4 + ((z ^ 1) if (dp + step // 2) % 2 == 0 else 3 - z)
                pairs.append((dp * 8 + hi * 4 + z, dp * 8 + to))
    return lax.ppermute(x, ("dp", "tp"), pairs)


def shards(queries, kv_pool, span_start, page_table, fire_slope, fire_shift, fire_mix, out_weight):
    units = jnp.concatenate(
        [fire_slope[None], fire_shift[None], jnp.zeros((6, HIDDEN), jnp.float32), fire_mix.T / SCALE]
    )
    units = jnp.pad(units, ((0, 0), (0, 128 - HIDDEN)))
    f32, bf16 = jnp.float32, jnp.bfloat16
    chunks = queries.shape[0] // CHUNK
    mine, got, got_x, part, outs = ([None] * chunks for _ in range(5))

    def along_x(c):
        got[c] = swap(mine[c][0], 0)
        return (mine[c][1].astype(f32) + got[c][2:].astype(f32)).astype(bf16)

    def along_z(c, crossed):
        got_x[c] = swap(crossed, 1)
        part[c] = [
            mine[c][2][n].astype(f32) + got[c][n].astype(f32) + got_x[c][n].astype(f32)
            for n in range(2)
        ]
        return part[c][1].astype(bf16)

    crossed, last = [None] * chunks, [None] * chunks
    for c in range(chunks):
        after = []
        if c >= 1:
            after.append(mine[c - 1][0])
        if c >= 2:
            crossed[c - 2] = along_x(c - 2)
            after.append(crossed[c - 2])
        if c >= 3:
            last[c - 3] = along_z(c - 3, crossed[c - 3])
            after.append(last[c - 3])
        mine[c] = partial_sums(c, span_start, page_table, units, queries, kv_pool, out_weight, after)
    for c in range(chunks):
        if crossed[c] is None:
            crossed[c] = along_x(c)
        if last[c] is None:
            last[c] = along_z(c, crossed[c])
        outs[c] = (part[c][0] + swap(last[c], 2).astype(f32)).astype(bf16)
    return jnp.concatenate(outs, axis=0)


def solution(mesh):
    in_specs = (
        P("dp", "tp"),
        P("dp", None, "tp"),
        P("dp"),
        P("dp", None),
        P(),
        P(),
        P(None, "tp"),
        P("tp", None),
    )
    out_specs = P("dp", "tp")
    return jax.shard_map(shards, mesh=mesh, in_specs=in_specs, out_specs=out_specs, check_vma=False)
```

```python
import functools
import math

import jax
import jax.numpy as jnp
from jax import lax
from jax.experimental import pallas as pl
from jax.experimental.pallas import tpu as pltpu
from jax.sharding import PartitionSpec as P

HEAD_DIM = 128
PAGE = 128
HEADS = 8
HIDDEN = 32
CHUNK = 128
KEYS = 256
GROUP = 32
WIDE = HEADS * CHUNK
COLUMNS = 1024
TILES = 2048 // KEYS
THRESHOLD = 32
NEG = -1e30
SCALE = HEAD_DIM**-0.5
LOG2E = math.log2(math.e)
TO_EXP2 = SCALE * LOG2E
SUMS = 16
MIB = 1 << 20
LIMIT = 50


def column_blocks():
    me = lax.axis_index("tp")
    core = lax.rem(lax.axis_index("dp"), 2)
    hi, z = me // 4, lax.rem(me, 4)
    flip, mirror = z + 1 - 2 * lax.rem(z, 2), 3 - z
    first = jnp.where(core == 0, flip, mirror)
    second = jnp.where(core == 0, mirror, flip)
    both = 3 - first
    both = jnp.where(core == 0, 3 - flip, mirror + 1 - 2 * lax.rem(mirror, 2))
    own, other = hi * 4, (1 - hi) * 4
    return [
        own + first, own + both, other + first, other + both,
        other + z, other + second, own + z, own + second,
    ]


def attention(
    chunk, params, slope_ref, shift_ref, mix_ref, q_ref, kv_ref, qt, acc, peak,
    scores, probs, scale, xs, lines, bits, kinks, att,
):
    start_ref, table_ref, slopes, shifts, mixes = params
    row0 = (start_ref[0] + chunk) * PAGE
    for h in range(HEADS):
        columns = slice(h * 128, (h + 1) * 128)
        scaled = q_ref[:, columns].astype(jnp.float32).T * TO_EXP2
        upper = scaled.astype(jnp.bfloat16)
        qt[:128, columns] = upper
        qt[128:, columns] = (scaled - upper.astype(jnp.float32)).astype(jnp.bfloat16)
    acc[...] = jnp.zeros_like(acc)
    peak[...] = jnp.full_like(peak, NEG)
    probs[1][...] = jnp.zeros_like(probs[1])
    scale[1][...] = jnp.zeros_like(scale[1])
    rows = row0 + lax.broadcasted_iota(jnp.int32, (1, CHUNK), 1)
    rec = 1.0 / jnp.log(1.0 + jnp.maximum(rows, THRESHOLD).astype(jnp.float32))
    ahead = lax.broadcasted_iota(jnp.int32, (KEYS, CHUNK), 1) - lax.broadcasted_iota(
        jnp.int32, (KEYS, CHUNK), 0
    )
    pages = KEYS // PAGE
    tiles = (start_ref[0] + chunk + pages) // pages

    def slots(b):
        return [table_ref[0, jnp.minimum(b * pages + n, 15)] for n in range(pages)]

    gaps = row0 - KEYS * lax.broadcasted_iota(jnp.int32, (TILES, HIDDEN), 0)
    least_log = jnp.log(1.0 + jnp.maximum(gaps - (KEYS - 1), 0).astype(jnp.float32))
    most_log = jnp.log(1.0 + jnp.maximum(gaps + (CHUNK - 1), 0).astype(jnp.float32))
    low = least_log * (jnp.min(rec, axis=1, keepdims=True) * (1 - 1e-5))
    high = most_log * (jnp.max(rec, axis=1, keepdims=True) * (1 + 1e-5))
    slope, shift, mix = slope_ref[...], shift_ref[...], mix_ref[...] * LOG2E
    at_low, at_high = slope * low + shift, slope * high + shift
    least, most = jnp.minimum(at_low, at_high), jnp.maximum(at_low, at_high)
    unit = lax.broadcasted_iota(jnp.int32, (TILES, HIDDEN), 1)
    weight = jnp.left_shift(1, unit & 15).astype(jnp.float32)
    weight = jnp.where((least < 0) & (most > 0), weight, 0.0)
    weights = jnp.where(unit < 16, weight, 0.0), jnp.where(unit < 16, 0.0, weight)
    shift_on, slope_on = jnp.where(least >= 0, shift, 0.0), jnp.where(least >= 0, slope, 0.0)
    for b in range(TILES):
        for n, on in enumerate((shift_on, slope_on)):
            line = jnp.sum(mix * on[b : b + 1], axis=1, keepdims=True)
            lines[b, n] = jnp.broadcast_to(line, (HEADS, CHUNK))
            bits[b, n] = jnp.sum(weights[n][b : b + 1]).astype(jnp.int32)

    def score(b, slot):
        k = jnp.concatenate([kv_ref[s, :, :128] for s in slots(b)], axis=0)
        k = jnp.concatenate([k, k], axis=1)
        for g in range(HEADS // 2):
            columns = slice(g * 256, (g + 1) * 256)
            scores[slot][:, columns] = jnp.dot(k, qt[:, columns], preferred_element_type=jnp.float32)
        gap = row0 - b * KEYS
        xs[slot][...] = jnp.log(1.0 + jnp.maximum(ahead + gap, 0).astype(jnp.float32)) * rec

    def mend(b, slot):
        gap = row0 - b * KEYS
        halves = bits[jnp.minimum(b, TILES - 1), 0], bits[jnp.minimum(b, TILES - 1), 1]

        @pl.when((halves[0] + halves[1] > 0) | (gap < KEYS - 1))
        def _():
            bent = jnp.int32(0)
            for f in range(HIDDEN):
                kinks[bent] = f
                bent = bent + (lax.shift_right_logical(halves[f // 16], f % 16) & 1)
            kinks[bent] = 0

            def group(n, carry):
                at = pl.ds(pl.multiple_of(n * GROUP, GROUP), GROUP)
                x = xs[slot][at, :]

                def unit(e, terms):
                    f, g = kinks[2 * e], kinks[2 * e + 1]
                    second = jnp.where(2 * e + 1 < bent, LOG2E, 0.0)
                    one = jnp.maximum((slopes[f] * LOG2E) * x + shifts[f] * LOG2E, 0.0)
                    two = jnp.maximum((slopes[g] * second) * x + shifts[g] * second, 0.0)
                    return tuple(
                        t + (mixes[h, f] * one + mixes[h, g] * two)
                        for h, t in enumerate(terms)
                    )

                terms = tuple(scores[slot][at, h * 128 : (h + 1) * 128] for h in range(HEADS))
                unseen = gap - n * GROUP + CHUNK - 1 < 0
                terms = lax.fori_loop(0, jnp.where(unseen, 0, (bent + 1) // 2), unit, terms)
                seen = ahead[:GROUP] + (gap - n * GROUP) >= 0
                for h in range(HEADS):
                    scores[slot][at, h * 128 : (h + 1) * 128] = jnp.where(seen, terms[h], NEG)
                return carry

            lax.fori_loop(0, KEYS // GROUP, group, 0)

    def weigh(b, slot):
        b = jnp.minimum(b, TILES - 1)
        for h in range(HEADS):
            columns = slice(h * 128, (h + 1) * 128)
            flat = lines[b, 0, h : h + 1]
            t = scores[slot][:, columns] + lines[b, 1, h : h + 1] * xs[slot][...]
            before = peak[h : h + 1]
            after = jnp.maximum(before, jnp.max(t, axis=0, keepdims=True) + flat)
            factor = jnp.exp2(before - after)
            p = jnp.exp2(t - (after - flat))
            peak[h : h + 1] = after
            scale[slot][:, columns] = factor
            probs[slot][:, columns] = p.astype(jnp.bfloat16)

    def gather(b, slot):
        vt = jnp.concatenate([kv_ref[s, :, 128:].T for s in slots(b)], axis=1)
        vt = jnp.concatenate([vt, jnp.ones((SUMS, KEYS), jnp.bfloat16)], axis=0)
        for g in range(HEADS // 2):
            columns = slice(g * 256, (g + 1) * 256)
            update = jnp.dot(vt, probs[slot][:, columns], preferred_element_type=jnp.float32)
            acc[:, columns] = acc[:, columns] * scale[slot][:, columns] + update

    def step(b, slot):
        mend(b, slot)
        score(b + 1, 1 - slot)
        gather(jnp.maximum(b - 1, 0), 1 - slot)
        weigh(b, slot)

    def tile(b, carry):
        for slot in range(2):
            pl.when(b % 2 == slot)(functools.partial(step, b, slot))
        return carry

    score(0, 0)
    lax.fori_loop(0, tiles, tile, 0)
    for slot in range(2):
        pl.when(tiles % 2 != slot)(functools.partial(gather, tiles - 1, slot))
    for h in range(HEADS):
        columns = slice(h * 128, (h + 1) * 128)
        total = acc[128:129, columns]
        att[:, columns] = (acc[:128, columns] / total).T.astype(jnp.bfloat16)


def kernel(chunk, attends, rows, keeps, waits, *refs):
    refs = list(refs)
    take = lambda n: [refs.pop(0) for _ in range(n)]
    inputs = take(10) if attends else []
    (w_ref,) = take(1)
    given = take(1) if rows > CHUNK or not attends else []
    take(waits)
    sends = take(1) if attends else []
    kept = [take(2) for _ in range(rows // CHUNK)] if keeps else []
    handed = [] if keeps else take(1)
    att, wbuf, stage, fetched, stored = take(5)
    blocks = column_blocks()
    first, last = (0 if attends else 4), (8 if keeps else 4)

    def fetch(n):
        columns = pl.ds(pl.multiple_of(blocks[n] * COLUMNS, COLUMNS), COLUMNS)
        return pltpu.make_async_copy(w_ref.at[:, columns], wbuf.at[n - first], fetched.at[n - first])

    for n in range(first, last):
        fetch(n).start()
    if given:
        att[:CHUNK] = given[0][...]
    own = slice(rows - CHUNK, rows)
    if attends:
        qt, acc, peak, s0, s1, p0, p1, f0, f1, x0, x1, lines, bits, kinks = take(14)
        attention(
            chunk, inputs[:5], *inputs[5:], qt, acc, peak, (s0, s1), (p0, p1), (f0, f1),
            (x0, x1), lines, bits, kinks, att.at[own],
        )
    copies = []

    def store(start, count, ref):
        n = len(copies)
        copies.append(pltpu.make_async_copy(stage.at[start : start + count], ref, stored.at[n]))
        copies[-1].start()

    if attends:
        for n in range(4):
            fetch(n).wait()

        def send(n, carry):
            product = jnp.dot(att[own], wbuf[n], preferred_element_type=jnp.float32)
            stage[n] = product.astype(jnp.bfloat16)
            return carry

        lax.fori_loop(0, 4, send, 0)
        store(0, 4, sends[0])
    if not keeps:
        copies.append(pltpu.make_async_copy(att, handed[0], stored.at[1]))
        copies[-1].start()
    for half in range(2 if keeps else 0):
        for n in range(2):
            fetch(4 + 2 * half + n).wait()

        def keep(n, carry, half=half):
            product = jnp.dot(
                att[...], wbuf[4 - first + 2 * half + n], preferred_element_type=jnp.float32
            ).astype(jnp.bfloat16)
            for r in range(rows // CHUNK):
                stage[4 + 2 * half + n + 4 * r] = product[r * CHUNK : (r + 1) * CHUNK]
            return carry

        lax.fori_loop(0, 2, keep, 0)
        for r in range(rows // CHUNK):
            store(4 + 2 * half + 4 * r, 2, kept[r][half])
    for copy in copies:
        copy.wait()


def partial_sums(chunk, attends, keeps, w, inputs=(), given=(), after=()):
    smem = pl.BlockSpec(memory_space=pltpu.SMEM)
    anywhere = pl.BlockSpec(memory_space=pl.ANY)
    whole = pl.BlockSpec(memory_space=pltpu.VMEM)
    rows = CHUNK * (int(attends) + len(given))
    blocks = lambda n: jax.ShapeDtypeStruct((n, CHUNK, COLUMNS), jnp.bfloat16)
    wanted = 4 * (int(attends) + int(keeps))
    in_specs, out_shape, scratch = [], [], []
    if attends:
        in_specs += [smem] * 5 + [whole] * 3
        in_specs += [pl.BlockSpec((CHUNK, HEADS * 128), lambda i: (chunk, 0)), whole]
        out_shape += [blocks(4)]
        scratch += [
            pltpu.VMEM((256, WIDE), jnp.bfloat16),
            pltpu.VMEM((128 + SUMS, WIDE), jnp.float32),
            pltpu.VMEM((HEADS, CHUNK), jnp.float32),
        ]
        scratch += [pltpu.VMEM((KEYS, WIDE), jnp.float32)] * 2
        scratch += [pltpu.VMEM((KEYS, WIDE), jnp.bfloat16)] * 2
        scratch += [pltpu.VMEM((1, WIDE), jnp.float32)] * 2
        scratch += [pltpu.VMEM((KEYS, CHUNK), jnp.float32)] * 2
        scratch += [
            pltpu.VMEM((TILES, 2, HEADS, CHUNK), jnp.float32),
            pltpu.SMEM((TILES, 2), jnp.int32),
            pltpu.SMEM((HIDDEN + 1,), jnp.int32),
        ]
    in_specs += [anywhere] + [whole] * len(given) + [anywhere] * len(after)
    if keeps:
        out_shape += [blocks(2)] * (2 * rows // CHUNK)
    else:
        out_shape += [jax.ShapeDtypeStruct((CHUNK, HEADS * 128), jnp.bfloat16)]
    return pl.pallas_call(
        functools.partial(kernel, chunk, attends, rows, keeps, len(after)),
        grid=(1,),
        in_specs=in_specs,
        out_specs=[anywhere] * len(out_shape),
        out_shape=out_shape,
        scratch_shapes=[
            pltpu.VMEM((rows, HEADS * 128), jnp.bfloat16),
            pltpu.VMEM((wanted, HEADS * 128, COLUMNS), jnp.bfloat16),
            pltpu.VMEM((4 + 4 * rows // CHUNK, CHUNK, COLUMNS), jnp.bfloat16),
            pltpu.SemaphoreType.DMA((wanted,)),
            pltpu.SemaphoreType.DMA((5,)),
        ]
        + scratch,
        compiler_params=pltpu.CompilerParams(vmem_limit_bytes=(60 if chunk == 0 else LIMIT) * MIB),
        cost_estimate=pl.CostEstimate(
            flops=10 * 10**9 if attends else 4 * 10**9,
            bytes_accessed=wanted * 2 * MIB + 4 * MIB,
            transcendentals=CHUNK * 2048 * 8 if attends else 0,
        ),
        name=f"chunk{chunk}" if attends else f"rest{chunk}",
    )(*inputs, w, *given, *after)


def add(terms, after):
    arrays = [x for x, _, _ in terms]
    if after:
        arrays[0] = lax.optimization_barrier((arrays[0], *after))[0]
    total = 0.0
    for x, (_, first, last) in zip(arrays, terms):
        total = total + x[first:last].astype(jnp.float32)
    return total.astype(jnp.bfloat16)


def swap(x, step):
    pairs = []
    for dp in range(16):
        for hi in range(2):
            for z in range(4):
                if step == 1:
                    to = (1 - hi) * 4 + z
                else:
                    to = hi * 4 + ((z ^ 1) if (dp + step // 2) % 2 == 0 else 3 - z)
                pairs.append((dp * 8 + hi * 4 + z, dp * 8 + to))
    return lax.ppermute(x, ("dp", "tp"), pairs)


def shards(queries, kv_pool, span_start, page_table, fire_slope, fire_shift, fire_mix, out_weight):
    mix = fire_mix.T
    inputs = (
        span_start, page_table, fire_slope, fire_shift, mix,
        fire_slope[None], fire_shift[None], mix, queries, kv_pool,
    )
    chunks = queries.shape[0] // CHUNK
    sent, cross, keep, got, got_x, got_z, crossed, last = ([None] * chunks for _ in range(8))

    def along_x(c, after=()):
        crossed[c] = add([(cross[c], 0, 2), (got[c], 2, 4)], after)
        got_x[c] = swap(crossed[c], 1)

    def along_z(c, after=()):
        last[c] = add([(keep[c], 1, 2), (got[c], 1, 2), (got_x[c], 1, 2)], after)
        got_z[c] = swap(last[c], 2)

    def run(c, attends, keeps, given=(), after=()):
        outs = partial_sums(c, attends, keeps, out_weight, inputs if attends else (), given, after)
        if attends:
            sent[c] = outs[0]
            got[c] = swap(sent[c], 0)
            outs = outs[1:]
        if keeps:
            for r, at in enumerate(range(c - (len(outs) // 2 - 1), c + 1)):
                cross[at], keep[at] = outs[2 * r : 2 * r + 2]
        return outs

    (held,) = run(0, True, False)
    run(1, True, True, [held], [sent[0]])
    along_x(0, [sent[1]])
    run(2, True, True, (), [crossed[0]])
    along_x(1, [sent[2]])
    along_z(0, [crossed[1]])
    (held,) = run(3, True, False, (), [last[0]])
    along_x(2, [sent[3]])
    along_z(1, [crossed[2]])
    run(3, False, True, [held], [last[1]])
    along_x(3)
    along_z(2, [crossed[3]])
    along_z(3, [last[2]])
    outs = [
        (
            keep[c][0].astype(jnp.float32)
            + got[c][0].astype(jnp.float32)
            + got_x[c][0].astype(jnp.float32)
            + got_z[c][0].astype(jnp.float32)
        ).astype(jnp.bfloat16)
        for c in range(chunks)
    ]
    return jnp.concatenate(outs, axis=0)


def solution(mesh):
    in_specs = (
        P("dp", "tp"),
        P("dp", None, "tp"),
        P("dp"),
        P("dp", None),
        P(),
        P(),
        P(None, "tp"),
        P("tp", None),
    )
    out_specs = P("dp", "tp")
    return jax.shard_map(shards, mesh=mesh, in_specs=in_specs, out_specs=out_specs, check_vma=False)
```

```python
import functools
import math

import jax
import jax.numpy as jnp
from jax import lax
from jax.experimental import pallas as pl
from jax.experimental.pallas import tpu as pltpu
from jax.sharding import PartitionSpec as P

HEAD_DIM = 128
PAGE = 128
HEADS = 8
HIDDEN = 32
CHUNK = 128
KEYS = 256
GROUP = 32
WIDE = HEADS * CHUNK
COLUMNS = 1024
TILES = 2048 // KEYS
THRESHOLD = 32
NEG = -1e30
SCALE = HEAD_DIM**-0.5
LOG2E = math.log2(math.e)
TO_EXP2 = SCALE * LOG2E
SUMS = 16
MIB = 1 << 20
LIMIT = 50


def column_blocks():
    me = lax.axis_index("tp")
    core = lax.rem(lax.axis_index("dp"), 2)
    hi, z = me // 4, lax.rem(me, 4)
    flip, mirror = z + 1 - 2 * lax.rem(z, 2), 3 - z
    first = jnp.where(core == 0, flip, mirror)
    second = jnp.where(core == 0, mirror, flip)
    both = 3 - first
    both = jnp.where(core == 0, 3 - flip, mirror + 1 - 2 * lax.rem(mirror, 2))
    own, other = hi * 4, (1 - hi) * 4
    return [
        own + first, own + both, other + first, other + both,
        other + z, other + second, own + z, own + second,
    ]


def attention(
    chunk, params, slope_ref, shift_ref, mix_ref, q_ref, kv_ref, qt, acc, peak,
    scores, probs, scale, xs, lines, bits, kinks, att,
):
    start_ref, table_ref, slopes, shifts, mixes = params
    row0 = (start_ref[0] + chunk) * PAGE
    for h in range(HEADS):
        columns = slice(h * 128, (h + 1) * 128)
        scaled = q_ref[:, columns].astype(jnp.float32).T * TO_EXP2
        upper = scaled.astype(jnp.bfloat16)
        qt[:128, columns] = upper
        qt[128:, columns] = (scaled - upper.astype(jnp.float32)).astype(jnp.bfloat16)
    acc[...] = jnp.zeros_like(acc)
    peak[...] = jnp.full_like(peak, NEG)
    probs[1][...] = jnp.zeros_like(probs[1])
    scale[1][...] = jnp.zeros_like(scale[1])
    rows = row0 + lax.broadcasted_iota(jnp.int32, (1, CHUNK), 1)
    rec = 1.0 / jnp.log(1.0 + jnp.maximum(rows, THRESHOLD).astype(jnp.float32))
    ahead = lax.broadcasted_iota(jnp.int32, (KEYS, CHUNK), 1) - lax.broadcasted_iota(
        jnp.int32, (KEYS, CHUNK), 0
    )
    pages = KEYS // PAGE
    tiles = (start_ref[0] + chunk + pages) // pages

    def slots(b):
        return [table_ref[0, jnp.minimum(b * pages + n, 15)] for n in range(pages)]

    gaps = row0 - KEYS * lax.broadcasted_iota(jnp.int32, (TILES, HIDDEN), 0)
    least_log = jnp.log(1.0 + jnp.maximum(gaps - (KEYS - 1), 0).astype(jnp.float32))
    most_log = jnp.log(1.0 + jnp.maximum(gaps + (CHUNK - 1), 0).astype(jnp.float32))
    low = least_log * (jnp.min(rec, axis=1, keepdims=True) * (1 - 1e-5))
    high = most_log * (jnp.max(rec, axis=1, keepdims=True) * (1 + 1e-5))
    slope, shift, mix = slope_ref[...], shift_ref[...], mix_ref[...] * LOG2E
    at_low, at_high = slope * low + shift, slope * high + shift
    least, most = jnp.minimum(at_low, at_high), jnp.maximum(at_low, at_high)
    unit = lax.broadcasted_iota(jnp.int32, (TILES, HIDDEN), 1)
    weight = jnp.left_shift(1, unit & 15).astype(jnp.float32)
    weight = jnp.where((least < 0) & (most > 0), weight, 0.0)
    weights = jnp.where(unit < 16, weight, 0.0), jnp.where(unit < 16, 0.0, weight)
    shift_on, slope_on = jnp.where(least >= 0, shift, 0.0), jnp.where(least >= 0, slope, 0.0)
    for b in range(TILES):
        for n, on in enumerate((shift_on, slope_on)):
            line = jnp.sum(mix * on[b : b + 1], axis=1, keepdims=True)
            lines[b, n] = jnp.broadcast_to(line, (HEADS, CHUNK))
            bits[b, n] = jnp.sum(weights[n][b : b + 1]).astype(jnp.int32)

    def score(b, slot):
        k = jnp.concatenate([kv_ref[s, :, :128] for s in slots(b)], axis=0)
        k = jnp.concatenate([k, k], axis=1)
        for g in range(HEADS // 2):
            columns = slice(g * 256, (g + 1) * 256)
            scores[slot][:, columns] = jnp.dot(k, qt[:, columns], preferred_element_type=jnp.float32)
        gap = row0 - b * KEYS
        xs[slot][...] = jnp.log(1.0 + jnp.maximum(ahead + gap, 0).astype(jnp.float32)) * rec

    def mend(b, slot):
        gap = row0 - b * KEYS
        halves = bits[jnp.minimum(b, TILES - 1), 0], bits[jnp.minimum(b, TILES - 1), 1]

        @pl.when((halves[0] + halves[1] > 0) | (gap < KEYS - 1))
        def _():
            bent = jnp.int32(0)
            for f in range(HIDDEN):
                kinks[bent] = f
                bent = bent + (lax.shift_right_logical(halves[f // 16], f % 16) & 1)
            kinks[bent] = 0

            def group(n, carry):
                at = pl.ds(pl.multiple_of(n * GROUP, GROUP), GROUP)
                x = xs[slot][at, :]

                def unit(e, terms):
                    f, g = kinks[2 * e], kinks[2 * e + 1]
                    second = jnp.where(2 * e + 1 < bent, LOG2E, 0.0)
                    one = jnp.maximum((slopes[f] * LOG2E) * x + shifts[f] * LOG2E, 0.0)
                    two = jnp.maximum((slopes[g] * second) * x + shifts[g] * second, 0.0)
                    return tuple(
                        t + (mixes[h, f] * one + mixes[h, g] * two)
                        for h, t in enumerate(terms)
                    )

                terms = tuple(scores[slot][at, h * 128 : (h + 1) * 128] for h in range(HEADS))
                unseen = gap - n * GROUP + CHUNK - 1 < 0
                terms = lax.fori_loop(0, jnp.where(unseen, 0, (bent + 1) // 2), unit, terms)
                seen = ahead[:GROUP] + (gap - n * GROUP) >= 0
                for h in range(HEADS):
                    scores[slot][at, h * 128 : (h + 1) * 128] = jnp.where(seen, terms[h], NEG)
                return carry

            lax.fori_loop(0, KEYS // GROUP, group, 0)

    def weigh(b, slot):
        b = jnp.minimum(b, TILES - 1)
        for h in range(HEADS):
            columns = slice(h * 128, (h + 1) * 128)
            flat = lines[b, 0, h : h + 1]
            t = scores[slot][:, columns] + lines[b, 1, h : h + 1] * xs[slot][...]
            before = peak[h : h + 1]
            after = jnp.maximum(before, jnp.max(t, axis=0, keepdims=True) + flat)
            factor = jnp.exp2(before - after)
            p = jnp.exp2(t - (after - flat))
            peak[h : h + 1] = after
            scale[slot][:, columns] = factor
            probs[slot][:, columns] = p.astype(jnp.bfloat16)

    def gather(b, slot):
        vt = jnp.concatenate([kv_ref[s, :, 128:].T for s in slots(b)], axis=1)
        vt = jnp.concatenate([vt, jnp.ones((SUMS, KEYS), jnp.bfloat16)], axis=0)
        for g in range(HEADS // 2):
            columns = slice(g * 256, (g + 1) * 256)
            update = jnp.dot(vt, probs[slot][:, columns], preferred_element_type=jnp.float32)
            acc[:, columns] = acc[:, columns] * scale[slot][:, columns] + update

    def step(b, slot):
        mend(b, slot)
        score(b + 1, 1 - slot)
        gather(jnp.maximum(b - 1, 0), 1 - slot)
        weigh(b, slot)

    def tile(b, carry):
        for slot in range(2):
            pl.when(b % 2 == slot)(functools.partial(step, b, slot))
        return carry

    score(0, 0)
    lax.fori_loop(0, tiles, tile, 0)
    for slot in range(2):
        pl.when(tiles % 2 != slot)(functools.partial(gather, tiles - 1, slot))
    for h in range(HEADS):
        columns = slice(h * 128, (h + 1) * 128)
        total = acc[128:129, columns]
        att[:, columns] = (acc[:128, columns] / total).T.astype(jnp.bfloat16)


def kernel(chunk, attends, rows, keeps, waits, *refs):
    refs = list(refs)
    take = lambda n: [refs.pop(0) for _ in range(n)]
    inputs = take(10) if attends else []
    (w_ref,) = take(1)
    given = take(rows // CHUNK - int(attends))
    take(waits)
    sends = take(1) if attends else []
    kept = [take(2) for _ in range(rows // CHUNK)] if keeps else []
    handed = [] if keeps else take(1)
    att, wbuf, stage, fetched, stored = take(5)
    blocks = column_blocks()
    first, last = (0 if attends else 4), (8 if keeps else 4)

    def fetch(n):
        columns = pl.ds(pl.multiple_of(blocks[n] * COLUMNS, COLUMNS), COLUMNS)
        return pltpu.make_async_copy(w_ref.at[:, columns], wbuf.at[n - first], fetched.at[n - first])

    for n in range(first, last):
        fetch(n).start()
    for r, ref in enumerate(given):
        att[r * CHUNK : (r + 1) * CHUNK] = ref[...]
    own = slice(rows - CHUNK, rows)
    if attends:
        qt, acc, peak, s0, s1, p0, p1, f0, f1, x0, x1, lines, bits, kinks = take(14)
        attention(
            chunk, inputs[:5], *inputs[5:], qt, acc, peak, (s0, s1), (p0, p1), (f0, f1),
            (x0, x1), lines, bits, kinks, att.at[own],
        )
    copies = []

    def store(start, count, ref):
        n = len(copies)
        copies.append(pltpu.make_async_copy(stage.at[start : start + count], ref, stored.at[n]))
        copies[-1].start()

    if attends:
        for n in range(4):
            fetch(n).wait()

        def send(n, carry):
            product = jnp.dot(att[own], wbuf[n], preferred_element_type=jnp.float32)
            stage[n] = product.astype(jnp.bfloat16)
            return carry

        lax.fori_loop(0, 4, send, 0)
        store(0, 4, sends[0])
    if not keeps:
        copies.append(pltpu.make_async_copy(att, handed[0], stored.at[1]))
        copies[-1].start()
    for half in range(2 if keeps else 0):
        for n in range(2):
            fetch(4 + 2 * half + n).wait()

        def keep(n, carry, half=half):
            product = jnp.dot(
                att[...], wbuf[4 - first + 2 * half + n], preferred_element_type=jnp.float32
            ).astype(jnp.bfloat16)
            for r in range(rows // CHUNK):
                stage[4 + 2 * half + n + 4 * r] = product[r * CHUNK : (r + 1) * CHUNK]
            return carry

        lax.fori_loop(0, 2, keep, 0)
        for r in range(rows // CHUNK):
            store(4 + 2 * half + 4 * r, 2, kept[r][half])
    for copy in copies:
        copy.wait()


def partial_sums(chunk, attends, keeps, w, inputs=(), given=(), after=()):
    smem = pl.BlockSpec(memory_space=pltpu.SMEM)
    anywhere = pl.BlockSpec(memory_space=pl.ANY)
    whole = pl.BlockSpec(memory_space=pltpu.VMEM)
    rows = CHUNK * (int(attends) + len(given))
    blocks = lambda n: jax.ShapeDtypeStruct((n, CHUNK, COLUMNS), jnp.bfloat16)
    wanted = 4 * (int(attends) + int(keeps))
    in_specs, out_shape, scratch = [], [], []
    if attends:
        in_specs += [smem] * 5 + [whole] * 3
        in_specs += [pl.BlockSpec((CHUNK, HEADS * 128), lambda i: (chunk, 0)), whole]
        out_shape += [blocks(4)]
        scratch += [
            pltpu.VMEM((256, WIDE), jnp.bfloat16),
            pltpu.VMEM((128 + SUMS, WIDE), jnp.float32),
            pltpu.VMEM((HEADS, CHUNK), jnp.float32),
        ]
        scratch += [pltpu.VMEM((KEYS, WIDE), jnp.float32)] * 2
        scratch += [pltpu.VMEM((KEYS, WIDE), jnp.bfloat16)] * 2
        scratch += [pltpu.VMEM((1, WIDE), jnp.float32)] * 2
        scratch += [pltpu.VMEM((KEYS, CHUNK), jnp.float32)] * 2
        scratch += [
            pltpu.VMEM((TILES, 2, HEADS, CHUNK), jnp.float32),
            pltpu.SMEM((TILES, 2), jnp.int32),
            pltpu.SMEM((HIDDEN + 1,), jnp.int32),
        ]
    in_specs += [anywhere] + [whole] * len(given) + [anywhere] * len(after)
    if keeps:
        out_shape += [blocks(2)] * (2 * rows // CHUNK)
    else:
        out_shape += [jax.ShapeDtypeStruct((CHUNK, HEADS * 128), jnp.bfloat16)]
    return pl.pallas_call(
        functools.partial(kernel, chunk, attends, rows, keeps, len(after)),
        grid=(1,),
        in_specs=in_specs,
        out_specs=[anywhere] * len(out_shape),
        out_shape=out_shape,
        scratch_shapes=[
            pltpu.VMEM((rows, HEADS * 128), jnp.bfloat16),
            pltpu.VMEM((wanted, HEADS * 128, COLUMNS), jnp.bfloat16),
            pltpu.VMEM((4 + 4 * rows // CHUNK, CHUNK, COLUMNS), jnp.bfloat16),
            pltpu.SemaphoreType.DMA((wanted,)),
            pltpu.SemaphoreType.DMA((5,)),
        ]
        + scratch,
        compiler_params=pltpu.CompilerParams(vmem_limit_bytes=(60 if chunk == 0 else LIMIT) * MIB),
        cost_estimate=pl.CostEstimate(
            flops=10 * 10**9 if attends else 4 * 10**9,
            bytes_accessed=wanted * 2 * MIB + 4 * MIB,
            transcendentals=CHUNK * 2048 * 8 if attends else 0,
        ),
        name=f"chunk{chunk}" if attends else f"rest{chunk}",
    )(*inputs, w, *given, *after)


def add(terms, after):
    arrays = [x for x, _, _ in terms]
    if after:
        arrays[0] = lax.optimization_barrier((arrays[0], *after))[0]
    total = 0.0
    for x, (_, first, last) in zip(arrays, terms):
        total = total + x[first:last].astype(jnp.float32)
    return total.astype(jnp.bfloat16)


def swap(x, step):
    pairs = []
    for dp in range(16):
        for hi in range(2):
            for z in range(4):
                if step == 1:
                    to = (1 - hi) * 4 + z
                else:
                    to = hi * 4 + ((z ^ 1) if (dp + step // 2) % 2 == 0 else 3 - z)
                pairs.append((dp * 8 + hi * 4 + z, dp * 8 + to))
    return lax.ppermute(x, ("dp", "tp"), pairs)


def shards(queries, kv_pool, span_start, page_table, fire_slope, fire_shift, fire_mix, out_weight):
    mix = fire_mix.T
    inputs = (
        span_start, page_table, fire_slope, fire_shift, mix,
        fire_slope[None], fire_shift[None], mix, queries, kv_pool,
    )
    chunks = queries.shape[0] // CHUNK
    sent, cross, keep, got, got_x, got_z, crossed, last = ([None] * chunks for _ in range(8))

    def along_x(c, after=()):
        crossed[c] = add([(cross[c], 0, 2), (got[c], 2, 4)], after)
        got_x[c] = swap(crossed[c], 1)

    def along_z(c, after=()):
        last[c] = add([(keep[c], 1, 2), (got[c], 1, 2), (got_x[c], 1, 2)], after)
        got_z[c] = swap(last[c], 2)

    def run(c, attends, keeps, given=(), after=()):
        outs = partial_sums(c, attends, keeps, out_weight, inputs if attends else (), given, after)
        if attends:
            sent[c] = outs[0]
            got[c] = swap(sent[c], 0)
            outs = outs[1:]
        if keeps:
            for r, at in enumerate(range(c - (len(outs) // 2 - 1), c + 1)):
                cross[at], keep[at] = outs[2 * r : 2 * r + 2]
        return outs

    (held,) = run(0, True, False)
    run(1, True, True, [held], [sent[0]])
    along_x(0, [sent[1]])
    (held,) = run(2, True, False, (), [crossed[0]])
    along_x(1, [sent[2]])
    along_z(0, [crossed[1]])
    held = [held, *run(3, True, False, (), [last[0]])]
    run(3, False, True, held, [sent[3]])
    along_x(2)
    along_z(1, [crossed[2]])
    along_x(3, [crossed[2]])
    along_z(2, [crossed[3]])
    along_z(3, [last[2]])
    outs = [
        (
            keep[c][0].astype(jnp.float32)
            + got[c][0].astype(jnp.float32)
            + got_x[c][0].astype(jnp.float32)
            + got_z[c][0].astype(jnp.float32)
        ).astype(jnp.bfloat16)
        for c in range(chunks)
    ]
    whole = jnp.concatenate(outs[:-1] + [jnp.zeros_like(outs[-1])], axis=0)
    return lax.dynamic_update_slice(whole, outs[-1], ((chunks - 1) * CHUNK, 0))


def solution(mesh):
    in_specs = (
        P("dp", "tp"),
        P("dp", None, "tp"),
        P("dp"),
        P("dp", None),
        P(),
        P(),
        P(None, "tp"),
        P("tp", None),
    )
    out_specs = P("dp", "tp")
    return jax.shard_map(shards, mesh=mesh, in_specs=in_specs, out_specs=out_specs, check_vma=False)
```

```python
import functools
import math

import jax
import jax.numpy as jnp
from jax import lax
from jax.experimental import pallas as pl
from jax.experimental.pallas import tpu as pltpu
from jax.sharding import PartitionSpec as P

HEAD_DIM = 128
PAGE = 128
HEADS = 8
HIDDEN = 32
CHUNK = 128
KEYS = 256
GROUP = 32
WIDE = HEADS * CHUNK
COLUMNS = 1024
TILES = 2048 // KEYS
THRESHOLD = 32
NEG = -1e30
SCALE = HEAD_DIM**-0.5
LOG2E = math.log2(math.e)
TO_EXP2 = SCALE * LOG2E
SUMS = 16
MIB = 1 << 20
LIMIT = 50


def column_blocks():
    me = lax.axis_index("tp")
    core = lax.rem(lax.axis_index("dp"), 2)
    hi, z = me // 4, lax.rem(me, 4)
    flip, mirror = z + 1 - 2 * lax.rem(z, 2), 3 - z
    first = jnp.where(core == 0, flip, mirror)
    second = jnp.where(core == 0, mirror, flip)
    both = 3 - first
    both = jnp.where(core == 0, 3 - flip, mirror + 1 - 2 * lax.rem(mirror, 2))
    own, other = hi * 4, (1 - hi) * 4
    return [
        own + first, own + both, other + first, other + both,
        other + z, other + second, own + z, own + second,
    ]


def attention(
    chunk, params, slope_ref, shift_ref, mix_ref, q_ref, kv_ref, qt, acc, peak,
    scores, probs, scale, xs, lines, bits, kinks, att,
):
    start_ref, table_ref, slopes, shifts, mixes = params
    row0 = (start_ref[0] + chunk) * PAGE
    for h in range(HEADS):
        columns = slice(h * 128, (h + 1) * 128)
        scaled = q_ref[:, columns].astype(jnp.float32).T * TO_EXP2
        upper = scaled.astype(jnp.bfloat16)
        qt[:128, columns] = upper
        qt[128:, columns] = (scaled - upper.astype(jnp.float32)).astype(jnp.bfloat16)
    acc[...] = jnp.zeros_like(acc)
    peak[...] = jnp.full_like(peak, NEG)
    probs[1][...] = jnp.zeros_like(probs[1])
    scale[1][...] = jnp.zeros_like(scale[1])
    rows = row0 + lax.broadcasted_iota(jnp.int32, (1, CHUNK), 1)
    rec = 1.0 / jnp.log(1.0 + jnp.maximum(rows, THRESHOLD).astype(jnp.float32))
    ahead = lax.broadcasted_iota(jnp.int32, (KEYS, CHUNK), 1) - lax.broadcasted_iota(
        jnp.int32, (KEYS, CHUNK), 0
    )
    pages = KEYS // PAGE
    tiles = (start_ref[0] + chunk + pages) // pages

    def slots(b):
        return [table_ref[0, jnp.minimum(b * pages + n, 15)] for n in range(pages)]

    gaps = row0 - KEYS * lax.broadcasted_iota(jnp.int32, (TILES, HIDDEN), 0)
    least_log = jnp.log(1.0 + jnp.maximum(gaps - (KEYS - 1), 0).astype(jnp.float32))
    most_log = jnp.log(1.0 + jnp.maximum(gaps + (CHUNK - 1), 0).astype(jnp.float32))
    low = least_log * (jnp.min(rec, axis=1, keepdims=True) * (1 - 1e-5))
    high = most_log * (jnp.max(rec, axis=1, keepdims=True) * (1 + 1e-5))
    slope, shift, mix = slope_ref[...], shift_ref[...], mix_ref[...] * LOG2E
    at_low, at_high = slope * low + shift, slope * high + shift
    least, most = jnp.minimum(at_low, at_high), jnp.maximum(at_low, at_high)
    unit = lax.broadcasted_iota(jnp.int32, (TILES, HIDDEN), 1)
    weight = jnp.left_shift(1, unit & 15).astype(jnp.float32)
    weight = jnp.where((least < 0) & (most > 0), weight, 0.0)
    weights = jnp.where(unit < 16, weight, 0.0), jnp.where(unit < 16, 0.0, weight)
    shift_on, slope_on = jnp.where(least >= 0, shift, 0.0), jnp.where(least >= 0, slope, 0.0)
    for b in range(TILES):
        for n, on in enumerate((shift_on, slope_on)):
            line = jnp.sum(mix * on[b : b + 1], axis=1, keepdims=True)
            lines[b, n] = jnp.broadcast_to(line, (HEADS, CHUNK))
            bits[b, n] = jnp.sum(weights[n][b : b + 1]).astype(jnp.int32)

    def score(b, slot):
        k = jnp.concatenate([kv_ref[s, :, :128] for s in slots(b)], axis=0)
        k = jnp.concatenate([k, k], axis=1)
        for g in range(HEADS // 2):
            columns = slice(g * 256, (g + 1) * 256)
            scores[slot][:, columns] = jnp.dot(k, qt[:, columns], preferred_element_type=jnp.float32)
        gap = row0 - b * KEYS
        xs[slot][...] = jnp.log(1.0 + jnp.maximum(ahead + gap, 0).astype(jnp.float32)) * rec

    def mend(b, slot):
        gap = row0 - b * KEYS
        halves = bits[jnp.minimum(b, TILES - 1), 0], bits[jnp.minimum(b, TILES - 1), 1]

        @pl.when((halves[0] + halves[1] > 0) | (gap < KEYS - 1))
        def _():
            bent = jnp.int32(0)
            for f in range(HIDDEN):
                kinks[bent] = f
                bent = bent + (lax.shift_right_logical(halves[f // 16], f % 16) & 1)
            kinks[bent] = 0

            def group(n, carry):
                at = pl.ds(pl.multiple_of(n * GROUP, GROUP), GROUP)
                x = xs[slot][at, :]

                def unit(e, terms):
                    f, g = kinks[2 * e], kinks[2 * e + 1]
                    second = jnp.where(2 * e + 1 < bent, LOG2E, 0.0)
                    one = jnp.maximum((slopes[f] * LOG2E) * x + shifts[f] * LOG2E, 0.0)
                    two = jnp.maximum((slopes[g] * second) * x + shifts[g] * second, 0.0)
                    return tuple(
                        t + (mixes[h, f] * one + mixes[h, g] * two)
                        for h, t in enumerate(terms)
                    )

                terms = tuple(scores[slot][at, h * 128 : (h + 1) * 128] for h in range(HEADS))
                unseen = gap - n * GROUP + CHUNK - 1 < 0
                terms = lax.fori_loop(0, jnp.where(unseen, 0, (bent + 1) // 2), unit, terms)
                seen = ahead[:GROUP] + (gap - n * GROUP) >= 0
                for h in range(HEADS):
                    scores[slot][at, h * 128 : (h + 1) * 128] = jnp.where(seen, terms[h], NEG)
                return carry

            lax.fori_loop(0, KEYS // GROUP, group, 0)

    def weigh(b, slot):
        b = jnp.minimum(b, TILES - 1)
        for h in range(HEADS):
            columns = slice(h * 128, (h + 1) * 128)
            flat = lines[b, 0, h : h + 1]
            t = scores[slot][:, columns] + lines[b, 1, h : h + 1] * xs[slot][...]
            before = peak[h : h + 1]
            after = jnp.maximum(before, jnp.max(t, axis=0, keepdims=True) + flat)
            factor = jnp.exp2(before - after)
            p = jnp.exp2(t - (after - flat))
            peak[h : h + 1] = after
            scale[slot][:, columns] = factor
            probs[slot][:, columns] = p.astype(jnp.bfloat16)

    def gather(b, slot):
        vt = jnp.concatenate([kv_ref[s, :, 128:].T for s in slots(b)], axis=1)
        vt = jnp.concatenate([vt, jnp.ones((SUMS, KEYS), jnp.bfloat16)], axis=0)
        for g in range(HEADS // 2):
            columns = slice(g * 256, (g + 1) * 256)
            update = jnp.dot(vt, probs[slot][:, columns], preferred_element_type=jnp.float32)
            acc[:, columns] = acc[:, columns] * scale[slot][:, columns] + update

    def step(b, slot):
        mend(b, slot)
        score(b + 1, 1 - slot)
        gather(jnp.maximum(b - 1, 0), 1 - slot)
        weigh(b, slot)

    def tile(b, carry):
        for slot in range(2):
            pl.when(b % 2 == slot)(functools.partial(step, b, slot))
        return carry

    score(0, 0)
    lax.fori_loop(0, tiles, tile, 0)
    for slot in range(2):
        pl.when(tiles % 2 != slot)(functools.partial(gather, tiles - 1, slot))
    for h in range(HEADS):
        columns = slice(h * 128, (h + 1) * 128)
        total = acc[128:129, columns]
        att[:, columns] = (acc[:128, columns] / total).T.astype(jnp.bfloat16)


def kernel(chunk, attends, rows, keeps, waits, *refs):
    refs = list(refs)
    take = lambda n: [refs.pop(0) for _ in range(n)]
    inputs = take(10) if attends else []
    (w_ref,) = take(1)
    given = take(rows // CHUNK - int(attends))
    take(waits)
    sends = take(1) if attends else []
    kept = [take(len(keeps)) for _ in range(rows // CHUNK)] if keeps else []
    handed = [] if keeps else take(1)
    att, wbuf, stage, fetched, stored = take(5)
    blocks = column_blocks()
    first = 0 if attends else 4 + 2 * keeps[0]
    last = 6 + 2 * keeps[-1] if keeps else 4

    def fetch(n):
        columns = pl.ds(pl.multiple_of(blocks[n] * COLUMNS, COLUMNS), COLUMNS)
        return pltpu.make_async_copy(w_ref.at[:, columns], wbuf.at[n - first], fetched.at[n - first])

    for n in range(first, last):
        fetch(n).start()
    for r, ref in enumerate(given):
        att[r * CHUNK : (r + 1) * CHUNK] = ref[...]
    own = slice(rows - CHUNK, rows)
    if attends:
        qt, acc, peak, s0, s1, p0, p1, f0, f1, x0, x1, lines, bits, kinks = take(14)
        attention(
            chunk, inputs[:5], *inputs[5:], qt, acc, peak, (s0, s1), (p0, p1), (f0, f1),
            (x0, x1), lines, bits, kinks, att.at[own],
        )
    copies = []

    def store(start, count, ref):
        n = len(copies)
        copies.append(pltpu.make_async_copy(stage.at[start : start + count], ref, stored.at[n]))
        copies[-1].start()

    if attends:
        for n in range(4):
            fetch(n).wait()

        def send(n, carry):
            product = jnp.dot(att[own], wbuf[n], preferred_element_type=jnp.float32)
            stage[n] = product.astype(jnp.bfloat16)
            return carry

        lax.fori_loop(0, 4, send, 0)
        store(0, 4, sends[0])
    if not keeps:
        copies.append(pltpu.make_async_copy(att, handed[0], stored.at[1]))
        copies[-1].start()
    for half in keeps:
        for n in range(2):
            fetch(4 + 2 * half + n).wait()

        def keep(n, carry, half=half):
            product = jnp.dot(
                att[...], wbuf[4 - first + 2 * half + n], preferred_element_type=jnp.float32
            ).astype(jnp.bfloat16)
            for r in range(rows // CHUNK):
                stage[4 + 2 * half + n + 4 * r] = product[r * CHUNK : (r + 1) * CHUNK]
            return carry

        lax.fori_loop(0, 2, keep, 0)
        for r in range(rows // CHUNK):
            store(4 + 2 * half + 4 * r, 2, kept[r][half - keeps[0]])
    for copy in copies:
        copy.wait()


def partial_sums(chunk, attends, keeps, w, inputs=(), given=(), after=()):
    smem = pl.BlockSpec(memory_space=pltpu.SMEM)
    anywhere = pl.BlockSpec(memory_space=pl.ANY)
    whole = pl.BlockSpec(memory_space=pltpu.VMEM)
    rows = CHUNK * (int(attends) + len(given))
    blocks = lambda n: jax.ShapeDtypeStruct((n, CHUNK, COLUMNS), jnp.bfloat16)
    wanted = 4 * int(attends) + 2 * len(keeps)
    in_specs, out_shape, scratch = [], [], []
    if attends:
        in_specs += [smem] * 5 + [whole] * 3
        in_specs += [pl.BlockSpec((CHUNK, HEADS * 128), lambda i: (chunk, 0)), whole]
        out_shape += [blocks(4)]
        scratch += [
            pltpu.VMEM((256, WIDE), jnp.bfloat16),
            pltpu.VMEM((128 + SUMS, WIDE), jnp.float32),
            pltpu.VMEM((HEADS, CHUNK), jnp.float32),
        ]
        scratch += [pltpu.VMEM((KEYS, WIDE), jnp.float32)] * 2
        scratch += [pltpu.VMEM((KEYS, WIDE), jnp.bfloat16)] * 2
        scratch += [pltpu.VMEM((1, WIDE), jnp.float32)] * 2
        scratch += [pltpu.VMEM((KEYS, CHUNK), jnp.float32)] * 2
        scratch += [
            pltpu.VMEM((TILES, 2, HEADS, CHUNK), jnp.float32),
            pltpu.SMEM((TILES, 2), jnp.int32),
            pltpu.SMEM((HIDDEN + 1,), jnp.int32),
        ]
    in_specs += [anywhere] + [whole] * len(given) + [anywhere] * len(after)
    if keeps:
        out_shape += [blocks(2)] * (len(keeps) * rows // CHUNK)
    else:
        out_shape += [jax.ShapeDtypeStruct((CHUNK, HEADS * 128), jnp.bfloat16)]
    return pl.pallas_call(
        functools.partial(kernel, chunk, attends, rows, keeps, len(after)),
        grid=(1,),
        in_specs=in_specs,
        out_specs=[anywhere] * len(out_shape),
        out_shape=out_shape,
        scratch_shapes=[
            pltpu.VMEM((rows, HEADS * 128), jnp.bfloat16),
            pltpu.VMEM((wanted, HEADS * 128, COLUMNS), jnp.bfloat16),
            pltpu.VMEM((4 + 4 * rows // CHUNK, CHUNK, COLUMNS), jnp.bfloat16),
            pltpu.SemaphoreType.DMA((wanted,)),
            pltpu.SemaphoreType.DMA((5,)),
        ]
        + scratch,
        compiler_params=pltpu.CompilerParams(vmem_limit_bytes=(60 if chunk == 0 else LIMIT) * MIB),
        cost_estimate=pl.CostEstimate(
            flops=10 * 10**9 if attends else 4 * 10**9,
            bytes_accessed=wanted * 2 * MIB + 4 * MIB,
            transcendentals=CHUNK * 2048 * 8 if attends else 0,
        ),
        name=f"chunk{chunk}" if attends else f"half{keeps[0]}",
    )(*inputs, w, *given, *after)


def add(terms, after):
    arrays = [x for x, _, _ in terms]
    if after:
        arrays[0] = lax.optimization_barrier((arrays[0], *after))[0]
    total = 0.0
    for x, (_, first, last) in zip(arrays, terms):
        total = total + x[first:last].astype(jnp.float32)
    return total.astype(jnp.bfloat16)


def swap(x, step):
    pairs = []
    for dp in range(16):
        for hi in range(2):
            for z in range(4):
                if step == 1:
                    to = (1 - hi) * 4 + z
                else:
                    to = hi * 4 + ((z ^ 1) if (dp + step // 2) % 2 == 0 else 3 - z)
                pairs.append((dp * 8 + hi * 4 + z, dp * 8 + to))
    return lax.ppermute(x, ("dp", "tp"), pairs)


def shards(queries, kv_pool, span_start, page_table, fire_slope, fire_shift, fire_mix, out_weight):
    mix = fire_mix.T
    inputs = (
        span_start, page_table, fire_slope, fire_shift, mix,
        fire_slope[None], fire_shift[None], mix, queries, kv_pool,
    )
    chunks = queries.shape[0] // CHUNK
    sent, cross, keep, got, got_x, got_z, crossed, last = ([None] * chunks for _ in range(8))

    def along_x(c, after=()):
        crossed[c] = add([(cross[c], 0, 2), (got[c], 2, 4)], after)
        got_x[c] = swap(crossed[c], 1)

    def along_z(c, after=()):
        last[c] = add([(keep[c], 1, 2), (got[c], 1, 2), (got_x[c], 1, 2)], after)
        got_z[c] = swap(last[c], 2)

    def run(c, attends, keeps, given=(), after=()):
        outs = partial_sums(c, attends, keeps, out_weight, inputs if attends else (), given, after)
        if attends:
            sent[c] = outs[0]
            got[c] = swap(sent[c], 0)
            outs = outs[1:]
        if keeps:
            count = len(outs) // len(keeps)
            for n, out in enumerate(outs):
                (cross, keep)[keeps[n % len(keeps)]][c + 1 - count + n // len(keeps)] = out
        return outs

    (held,) = run(0, True, ())
    run(1, True, (0, 1), [held], [sent[0]])
    along_x(0, [sent[1]])
    (held,) = run(2, True, (), (), [crossed[0]])
    held = [held, *run(3, True, (), (), [sent[2]])]
    along_x(1, [sent[3]])
    along_z(0, [crossed[1]])
    run(3, False, (0,), held, [last[0]])
    along_x(2)
    run(3, False, (1,), held, [crossed[2]])
    along_z(1, [keep[3]])
    along_x(3, [crossed[2]])
    along_z(2, [crossed[3]])
    along_z(3, [last[2]])
    outs = [
        (
            keep[c][0].astype(jnp.float32)
            + got[c][0].astype(jnp.float32)
            + got_x[c][0].astype(jnp.float32)
            + got_z[c][0].astype(jnp.float32)
        ).astype(jnp.bfloat16)
        for c in range(chunks)
    ]
    whole = jnp.concatenate(outs[:-1] + [jnp.zeros_like(outs[-1])], axis=0)
    return lax.dynamic_update_slice(whole, outs[-1], ((chunks - 1) * CHUNK, 0))


def solution(mesh):
    in_specs = (
        P("dp", "tp"),
        P("dp", None, "tp"),
        P("dp"),
        P("dp", None),
        P(),
        P(),
        P(None, "tp"),
        P("tp", None),
    )
    out_specs = P("dp", "tp")
    return jax.shard_map(shards, mesh=mesh, in_specs=in_specs, out_specs=out_specs, check_vma=False)
```

```python
import functools
import math

import jax
import jax.numpy as jnp
from jax import lax
from jax.experimental import pallas as pl
from jax.experimental.pallas import tpu as pltpu
from jax.sharding import PartitionSpec as P

HEAD_DIM = 128
PAGE = 128
HEADS = 8
HIDDEN = 32
CHUNK = 128
KEYS = 256
GROUP = 32
WIDE = HEADS * CHUNK
COLUMNS = 1024
TILES = 2048 // KEYS
THRESHOLD = 32
NEG = -1e30
SCALE = HEAD_DIM**-0.5
LOG2E = math.log2(math.e)
TO_EXP2 = SCALE * LOG2E
SUMS = 16
MIB = 1 << 20
LIMIT = 50


def column_blocks():
    me = lax.axis_index("tp")
    core = lax.rem(lax.axis_index("dp"), 2)
    hi, z = me // 4, lax.rem(me, 4)
    flip, mirror = z + 1 - 2 * lax.rem(z, 2), 3 - z
    first = jnp.where(core == 0, flip, mirror)
    second = jnp.where(core == 0, mirror, flip)
    both = 3 - first
    both = jnp.where(core == 0, 3 - flip, mirror + 1 - 2 * lax.rem(mirror, 2))
    own, other = hi * 4, (1 - hi) * 4
    return [
        own + first, own + both, other + first, other + both,
        other + z, other + second, own + z, own + second,
    ]


def attention(
    chunk, params, slope_ref, shift_ref, mix_ref, q_ref, kv_ref, qt, acc, peak,
    scores, probs, scale, xs, lines, bits, kinks, att,
):
    start_ref, table_ref, slopes, shifts, mixes = params
    row0 = (start_ref[0] + chunk) * PAGE
    for h in range(HEADS):
        columns = slice(h * 128, (h + 1) * 128)
        scaled = q_ref[:, columns].astype(jnp.float32).T * TO_EXP2
        upper = scaled.astype(jnp.bfloat16)
        qt[:128, columns] = upper
        qt[128:, columns] = (scaled - upper.astype(jnp.float32)).astype(jnp.bfloat16)
    acc[...] = jnp.zeros_like(acc)
    peak[...] = jnp.full_like(peak, NEG)
    probs[1][...] = jnp.zeros_like(probs[1])
    scale[1][...] = jnp.zeros_like(scale[1])
    rows = row0 + lax.broadcasted_iota(jnp.int32, (1, CHUNK), 1)
    rec = 1.0 / jnp.log(1.0 + jnp.maximum(rows, THRESHOLD).astype(jnp.float32))
    ahead = lax.broadcasted_iota(jnp.int32, (KEYS, CHUNK), 1) - lax.broadcasted_iota(
        jnp.int32, (KEYS, CHUNK), 0
    )
    pages = KEYS // PAGE
    tiles = (start_ref[0] + chunk + pages) // pages

    def slots(b):
        return [table_ref[0, jnp.minimum(b * pages + n, 15)] for n in range(pages)]

    gaps = row0 - KEYS * lax.broadcasted_iota(jnp.int32, (TILES, HIDDEN), 0)
    least_log = jnp.log(1.0 + jnp.maximum(gaps - (KEYS - 1), 0).astype(jnp.float32))
    most_log = jnp.log(1.0 + jnp.maximum(gaps + (CHUNK - 1), 0).astype(jnp.float32))
    low = least_log * (jnp.min(rec, axis=1, keepdims=True) * (1 - 1e-5))
    high = most_log * (jnp.max(rec, axis=1, keepdims=True) * (1 + 1e-5))
    slope, shift, mix = slope_ref[...], shift_ref[...], mix_ref[...] * LOG2E
    at_low, at_high = slope * low + shift, slope * high + shift
    least, most = jnp.minimum(at_low, at_high), jnp.maximum(at_low, at_high)
    unit = lax.broadcasted_iota(jnp.int32, (TILES, HIDDEN), 1)
    weight = jnp.left_shift(1, unit & 15).astype(jnp.float32)
    weight = jnp.where((least < 0) & (most > 0), weight, 0.0)
    weights = jnp.where(unit < 16, weight, 0.0), jnp.where(unit < 16, 0.0, weight)
    shift_on, slope_on = jnp.where(least >= 0, shift, 0.0), jnp.where(least >= 0, slope, 0.0)
    for b in range(TILES):
        for n, on in enumerate((shift_on, slope_on)):
            line = jnp.sum(mix * on[b : b + 1], axis=1, keepdims=True)
            lines[b, n] = jnp.broadcast_to(line, (HEADS, CHUNK))
            bits[b, n] = jnp.sum(weights[n][b : b + 1]).astype(jnp.int32)

    def score(b, slot):
        k = jnp.concatenate([kv_ref[s, :, :128] for s in slots(b)], axis=0)
        k = jnp.concatenate([k, k], axis=1)
        for g in range(HEADS // 2):
            columns = slice(g * 256, (g + 1) * 256)
            scores[slot][:, columns] = jnp.dot(k, qt[:, columns], preferred_element_type=jnp.float32)
        gap = row0 - b * KEYS
        xs[slot][...] = jnp.log(1.0 + jnp.maximum(ahead + gap, 0).astype(jnp.float32)) * rec

    def mend(b, slot):
        gap = row0 - b * KEYS
        halves = bits[jnp.minimum(b, TILES - 1), 0], bits[jnp.minimum(b, TILES - 1), 1]

        @pl.when((halves[0] + halves[1] > 0) | (gap < KEYS - 1))
        def _():
            bent = jnp.int32(0)
            for f in range(HIDDEN):
                kinks[bent] = f
                bent = bent + (lax.shift_right_logical(halves[f // 16], f % 16) & 1)
            kinks[bent] = 0

            def group(n, carry):
                at = pl.ds(pl.multiple_of(n * GROUP, GROUP), GROUP)
                x = xs[slot][at, :]

                def unit(e, terms):
                    f, g = kinks[2 * e], kinks[2 * e + 1]
                    second = jnp.where(2 * e + 1 < bent, LOG2E, 0.0)
                    one = jnp.maximum((slopes[f] * LOG2E) * x + shifts[f] * LOG2E, 0.0)
                    two = jnp.maximum((slopes[g] * second) * x + shifts[g] * second, 0.0)
                    return tuple(
                        t + (mixes[h, f] * one + mixes[h, g] * two)
                        for h, t in enumerate(terms)
                    )

                terms = tuple(scores[slot][at, h * 128 : (h + 1) * 128] for h in range(HEADS))
                unseen = gap - n * GROUP + CHUNK - 1 < 0
                terms = lax.fori_loop(0, jnp.where(unseen, 0, (bent + 1) // 2), unit, terms)
                seen = ahead[:GROUP] + (gap - n * GROUP) >= 0
                for h in range(HEADS):
                    scores[slot][at, h * 128 : (h + 1) * 128] = jnp.where(seen, terms[h], NEG)
                return carry

            lax.fori_loop(0, KEYS // GROUP, group, 0)

    def weigh(b, slot):
        b = jnp.minimum(b, TILES - 1)
        for h in range(HEADS):
            columns = slice(h * 128, (h + 1) * 128)
            flat = lines[b, 0, h : h + 1]
            t = scores[slot][:, columns] + lines[b, 1, h : h + 1] * xs[slot][...]
            before = peak[h : h + 1]
            after = jnp.maximum(before, jnp.max(t, axis=0, keepdims=True) + flat)
            factor = jnp.exp2(before - after)
            p = jnp.exp2(t - (after - flat))
            peak[h : h + 1] = after
            scale[slot][:, columns] = factor
            probs[slot][:, columns] = p.astype(jnp.bfloat16)

    def gather(b, slot):
        vt = jnp.concatenate([kv_ref[s, :, 128:].T for s in slots(b)], axis=1)
        vt = jnp.concatenate([vt, jnp.ones((SUMS, KEYS), jnp.bfloat16)], axis=0)
        for g in range(HEADS // 2):
            columns = slice(g * 256, (g + 1) * 256)
            update = jnp.dot(vt, probs[slot][:, columns], preferred_element_type=jnp.float32)
            acc[:, columns] = acc[:, columns] * scale[slot][:, columns] + update

    def step(b, slot):
        mend(b, slot)
        score(b + 1, 1 - slot)
        gather(jnp.maximum(b - 1, 0), 1 - slot)
        weigh(b, slot)

    def tile(b, carry):
        for slot in range(2):
            pl.when(b % 2 == slot)(functools.partial(step, b, slot))
        return carry

    score(0, 0)
    lax.fori_loop(0, tiles, tile, 0)
    for slot in range(2):
        pl.when(tiles % 2 != slot)(functools.partial(gather, tiles - 1, slot))
    for h in range(HEADS):
        columns = slice(h * 128, (h + 1) * 128)
        total = acc[128:129, columns]
        att[:, columns] = (acc[:128, columns] / total).T.astype(jnp.bfloat16)


def kernel(chunk, attends, rows, keeps, waits, *refs):
    refs = list(refs)
    take = lambda n: [refs.pop(0) for _ in range(n)]
    inputs = take(10) if attends else []
    (w_ref,) = take(1)
    given = take(rows // CHUNK - int(attends))
    take(waits)
    sends = take(1) if attends else []
    kept = [take(2) for _ in range(rows // CHUNK)] if keeps else []
    handed = [] if keeps else take(1)
    att, wbuf, stage, fetched, stored = take(5)
    blocks = column_blocks()
    first, last = (0 if attends else 4), (8 if keeps else 4)

    def fetch(n):
        columns = pl.ds(pl.multiple_of(blocks[n] * COLUMNS, COLUMNS), COLUMNS)
        return pltpu.make_async_copy(w_ref.at[:, columns], wbuf.at[n - first], fetched.at[n - first])

    for n in range(first, last):
        fetch(n).start()
    for r, ref in enumerate(given):
        att[r * CHUNK : (r + 1) * CHUNK] = ref[...]
    own = slice(rows - CHUNK, rows)
    if attends:
        qt, acc, peak, s0, s1, p0, p1, f0, f1, x0, x1, lines, bits, kinks = take(14)
        attention(
            chunk, inputs[:5], *inputs[5:], qt, acc, peak, (s0, s1), (p0, p1), (f0, f1),
            (x0, x1), lines, bits, kinks, att.at[own],
        )
    copies = []

    def store(start, count, ref):
        n = len(copies)
        copies.append(pltpu.make_async_copy(stage.at[start : start + count], ref, stored.at[n]))
        copies[-1].start()

    if attends:
        for n in range(4):
            fetch(n).wait()

        def send(n, carry):
            product = jnp.dot(att[own], wbuf[n], preferred_element_type=jnp.float32)
            stage[n] = product.astype(jnp.bfloat16)
            return carry

        lax.fori_loop(0, 4, send, 0)
        store(0, 4, sends[0])
    if not keeps:
        copies.append(pltpu.make_async_copy(att, handed[0], stored.at[1]))
        copies[-1].start()
    for half in range(2 if keeps else 0):
        for n in range(2):
            fetch(4 + 2 * half + n).wait()

        def keep(n, carry, half=half):
            product = jnp.dot(
                att[...], wbuf[4 - first + 2 * half + n], preferred_element_type=jnp.float32
            ).astype(jnp.bfloat16)
            for r in range(rows // CHUNK):
                stage[4 + 2 * half + n + 4 * r] = product[r * CHUNK : (r + 1) * CHUNK]
            return carry

        lax.fori_loop(0, 2, keep, 0)
        for r in range(rows // CHUNK):
            store(4 + 2 * half + 4 * r, 2, kept[r][half])
    for copy in copies:
        copy.wait()


def partial_sums(chunk, attends, keeps, w, inputs=(), given=(), after=()):
    smem = pl.BlockSpec(memory_space=pltpu.SMEM)
    anywhere = pl.BlockSpec(memory_space=pl.ANY)
    whole = pl.BlockSpec(memory_space=pltpu.VMEM)
    rows = CHUNK * (int(attends) + len(given))
    blocks = lambda n: jax.ShapeDtypeStruct((n, CHUNK, COLUMNS), jnp.bfloat16)
    wanted = 4 * (int(attends) + int(keeps))
    in_specs, out_shape, scratch = [], [], []
    if attends:
        in_specs += [smem] * 5 + [whole] * 3
        in_specs += [pl.BlockSpec((CHUNK, HEADS * 128), lambda i: (chunk, 0)), whole]
        out_shape += [blocks(4)]
        scratch += [
            pltpu.VMEM((256, WIDE), jnp.bfloat16),
            pltpu.VMEM((128 + SUMS, WIDE), jnp.float32),
            pltpu.VMEM((HEADS, CHUNK), jnp.float32),
        ]
        scratch += [pltpu.VMEM((KEYS, WIDE), jnp.float32)] * 2
        scratch += [pltpu.VMEM((KEYS, WIDE), jnp.bfloat16)] * 2
        scratch += [pltpu.VMEM((1, WIDE), jnp.float32)] * 2
        scratch += [pltpu.VMEM((KEYS, CHUNK), jnp.float32)] * 2
        scratch += [
            pltpu.VMEM((TILES, 2, HEADS, CHUNK), jnp.float32),
            pltpu.SMEM((TILES, 2), jnp.int32),
            pltpu.SMEM((HIDDEN + 1,), jnp.int32),
        ]
    in_specs += [anywhere] + [whole] * len(given) + [anywhere] * len(after)
    if keeps:
        out_shape += [blocks(2)] * (2 * rows // CHUNK)
    else:
        out_shape += [jax.ShapeDtypeStruct((CHUNK, HEADS * 128), jnp.bfloat16)]
    return pl.pallas_call(
        functools.partial(kernel, chunk, attends, rows, keeps, len(after)),
        grid=(1,),
        in_specs=in_specs,
        out_specs=[anywhere] * len(out_shape),
        out_shape=out_shape,
        scratch_shapes=[
            pltpu.VMEM((rows, HEADS * 128), jnp.bfloat16),
            pltpu.VMEM((wanted, HEADS * 128, COLUMNS), jnp.bfloat16),
            pltpu.VMEM((4 + 4 * rows // CHUNK, CHUNK, COLUMNS), jnp.bfloat16),
            pltpu.SemaphoreType.DMA((wanted,)),
            pltpu.SemaphoreType.DMA((5,)),
        ]
        + scratch,
        compiler_params=pltpu.CompilerParams(vmem_limit_bytes=(60 if chunk == 0 else LIMIT) * MIB),
        cost_estimate=pl.CostEstimate(
            flops=10 * 10**9 if attends else 4 * 10**9,
            bytes_accessed=wanted * 2 * MIB + 4 * MIB,
            transcendentals=CHUNK * 2048 * 8 if attends else 0,
        ),
        name=f"chunk{chunk}" if attends else f"rest{chunk}",
    )(*inputs, w, *given, *after)


def add(terms, after):
    arrays = [x for x, _, _ in terms]
    if after:
        arrays[0] = lax.optimization_barrier((arrays[0], *after))[0]
    total = 0.0
    for x, (_, first, last) in zip(arrays, terms):
        total = total + x[first:last].astype(jnp.float32)
    return total.astype(jnp.bfloat16)


def swap(x, step):
    pairs = []
    for dp in range(16):
        for hi in range(2):
            for z in range(4):
                if step == 1:
                    to = (1 - hi) * 4 + z
                else:
                    to = hi * 4 + ((z ^ 1) if (dp + step // 2) % 2 == 0 else 3 - z)
                pairs.append((dp * 8 + hi * 4 + z, dp * 8 + to))
    return lax.ppermute(x, ("dp", "tp"), pairs)


def shards(queries, kv_pool, span_start, page_table, fire_slope, fire_shift, fire_mix, out_weight):
    mix = fire_mix.T
    inputs = (
        span_start, page_table, fire_slope, fire_shift, mix,
        fire_slope[None], fire_shift[None], mix, queries, kv_pool,
    )
    chunks = queries.shape[0] // CHUNK
    sent, cross, keep, got, got_x, got_z, crossed, last = ([None] * chunks for _ in range(8))

    def along_x(c, after=()):
        crossed[c] = add([(cross[c], 0, 2), (got[c], 2, 4)], after)
        got_x[c] = swap(crossed[c], 1)

    def along_z(c, after=()):
        last[c] = add([(keep[c], 1, 2), (got[c], 1, 2), (got_x[c], 1, 2)], after)
        got_z[c] = swap(last[c], 2)

    def run(c, attends, keeps, given=(), after=()):
        outs = partial_sums(c, attends, keeps, out_weight, inputs if attends else (), given, after)
        if attends:
            sent[c] = outs[0]
            got[c] = swap(sent[c], 0)
            outs = outs[1:]
        if keeps:
            for r, at in enumerate(range(c - (len(outs) // 2 - 1), c + 1)):
                cross[at], keep[at] = outs[2 * r : 2 * r + 2]
        return outs

    (held,) = run(0, True, False)
    run(1, True, True, [held], [sent[0]])
    along_x(0, [sent[1]])
    (held,) = run(2, True, False, (), [crossed[0]])
    held = [held, *run(3, True, False, (), [sent[2]])]
    along_x(1, [sent[3]])
    along_z(0, [crossed[1]])
    run(3, False, True, held, [last[0]])
    along_x(2)
    along_z(1, [crossed[2]])
    along_x(3, [crossed[2]])
    along_z(2, [crossed[3]])
    along_z(3, [last[2]])
    outs = [
        (
            keep[c][0].astype(jnp.float32)
            + got[c][0].astype(jnp.float32)
            + got_x[c][0].astype(jnp.float32)
            + got_z[c][0].astype(jnp.float32)
        ).astype(jnp.bfloat16)
        for c in range(chunks)
    ]
    whole = jnp.concatenate(outs[:-1] + [jnp.zeros_like(outs[-1])], axis=0)
    return lax.dynamic_update_slice(whole, outs[-1], ((chunks - 1) * CHUNK, 0))


def solution(mesh):
    in_specs = (
        P("dp", "tp"),
        P("dp", None, "tp"),
        P("dp"),
        P("dp", None),
        P(),
        P(),
        P(None, "tp"),
        P("tp", None),
    )
    out_specs = P("dp", "tp")
    return jax.shard_map(shards, mesh=mesh, in_specs=in_specs, out_specs=out_specs, check_vma=False)
```
